128 devices in a mesh: prow: 8 (over y, core), pcol: 16 (over z, x).
Axes of the slice: x: 4, y: 4, z: 4, core: 2. Of those that a mesh axis runs over, the one named last changes fastest.
Arguments:
- rhs_blocks: float32 [22, 2048, 512], P(None, 'prow'), may hold values from -6 to 6
- factor_tiles: bfloat16 [22, 2048, 6, 2048], P(None, 'prow', None, 'pcol'), may hold values from -0.0546875 to 0.0546875
- tile_scale: float32 [22, 6], replicated, may hold values from 0.5 to 2
- diag_inverse: bfloat16 [6, 2048, 2048], P(None, None, 'prow'), may hold values from -1.5 to 1.5, as said below
Outputs:
- solved_blocks: float32 [6, 2048, 512], P(None, 'pcol')
- trailing_rhs: float32 [16, 2048, 512], P(None, 'prow')
The draws below stay inside these ranges and needn't reach their ends.
Inputs may be any that keep to these rules, and one draw needn't show every extreme that they name: `diag_inverse`: each block is zero above its diagonal.
All inputs are finite; a program needn't handle non-finite values.
Results may differ from the reference program's by a relative error of at most 0.0003.
Values sent between devices are 32-bit elements; how exact they have to be, the bound alone decides.
No kernel may reach another device: no remote copies, remote signals or barrier semaphores. Data moves between devices by JAX's collectives and lax.ppermute only.
A program may use at most 192 MiB of HBM per device.

```python
import math
import jax
import jax.numpy as jnp
from jax import lax

NB = 2048
RHS = 512
STEPS = 6
RBLK = 22


def draw_diag_inverse(key, part):
    key = jax.random.fold_in(key, 7)
    first_key, second_key = jax.random.split(key)
    positions = jnp.arange(NB)
    lower = positions[:, None] > positions[None, :]
    identity = (positions[:, None] == positions[None, :]).astype(jnp.float32)
    off_part = jax.random.normal(first_key, (STEPS, NB, NB), jnp.float32) * (0.7 / math.sqrt(NB))
    diag_part = jax.random.uniform(second_key, (STEPS, NB), jnp.float32, 0.7, 1.3)
    matrix = jnp.where(lower[None], off_part, 0.0) + diag_part[:, :, None] * identity[None]
    return matrix.astype(jnp.bfloat16)


def shard_levels(own_key, dims, pieces, least, top_value):
    factor_of = 1.0
    for dim, blocks in pieces:
        draws = jax.random.uniform(jax.random.fold_in(jax.random.fold_in(own_key, 6), dim), (blocks,), jnp.float32, least / len(pieces), top_value / len(pieces))
        factor_of = factor_of * jnp.repeat(jnp.exp(draws), dims[dim] // blocks).reshape((-1,) + (1,) * (len(dims) - 1 - dim))
    return factor_of


def centred(key, dims, scale, most, shards=(), kind=jnp.bfloat16):
    array = jax.random.normal(key, dims, jnp.float32) * scale
    if len(shards) > 0:
        array = shard_levels(key, dims, shards, -0.22, 0.18) * array
    return jnp.clip(array, min=-most, max=most).astype(kind)


def setup_inputs(seed: int = 0) -> dict:
    key_list = jax.random.split(jax.random.key(seed), 5)
    return {
        "rhs_blocks": centred(key_list[0], (RBLK, NB, RHS), 1.0, 6.0, ((1, 8),), jnp.float32),
        "factor_tiles": centred(key_list[1], (RBLK, NB, STEPS, NB), (NB * STEPS) ** -0.5, 0.0546875, ((1, 8), (3, 16))),
        "tile_scale": jnp.clip(jnp.exp(jax.random.uniform(key_list[2], (RBLK, STEPS), jnp.float32, math.log(0.5), math.log(2.0))), 0.5, 2.0),
        "diag_inverse": draw_diag_inverse(jax.random.fold_in(key_list[4], 71), 0),
    }


def reference(rhs_blocks, factor_tiles, tile_scale, diag_inverse):
    current = rhs_blocks
    solved = []
    for column in range(STEPS):
        solved_rows = jnp.dot(diag_inverse[column].astype(jnp.float32), current[column], precision=lax.Precision.HIGHEST)
        solved.append(solved_rows)
        weights = tile_scale[column + 1:, column]
        scaled_tiles = factor_tiles[column + 1:, :, column, :].astype(jnp.float32) * weights[:, None, None]
        update = jnp.einsum("sqj,jr->sqr", scaled_tiles, solved_rows, precision=lax.Precision.HIGHEST)
        current = jnp.concatenate([current[:column + 1], current[column + 1:] - update], axis=0)
    return jnp.stack(solved), current[STEPS:]
```

```python
import functools

import jax
import jax.numpy as jnp
from jax import lax
from jax.experimental import pallas as pl
from jax.experimental.pallas import tpu as pltpu
from jax.sharding import PartitionSpec as P

F32 = jnp.float32
BF16 = jnp.bfloat16
STEPS = 6
PAIRS = (((1, 0),), ((2, 0), (2, 1), (3, 0), (3, 1), (3, 2)), tuple((s, j) for s in (4, 5) for j in range(s)))


def split(value):
    high = value.astype(BF16)
    return high, (value - high.astype(F32)).astype(BF16)


def dot(a, b):
    return jnp.dot(a, b, preferred_element_type=F32)


def dot3(a, b):
    a_high, a_low = split(a)
    b_high, b_low = split(b)
    return dot(a_high, b_high) + (dot(a_high, b_low) + dot(a_low, b_high))


def full(shape):
    return pl.BlockSpec(shape, lambda *_: (0,) * len(shape))


def params(mib):
    return pltpu.CompilerParams(vmem_limit_bytes=mib << 20)


def store_gram(meta, product, keep, send, at):
    x, y, u = meta[0], meta[1], meta[2]
    for zz in range(4):
        for ex in range(4):
            chunk = zz * 4 + lax.rem(x + ex, 4)
            for ey in range(4):
                row = (chunk * 8 + lax.rem(y + ey, 4) * 2) * 16
                keep[ey, at + ex * 4 + zz] = product[pl.ds(pl.multiple_of(row + u * 16, 16), 16), :]
                send[ey, at + ex * 4 + zz] = product[pl.ds(pl.multiple_of(row + (1 - u) * 16, 16), 16), :]


def first_kernel(meta, scale, inverse, rhs, tile, keep, send, product):
    x, y, u, z = meta[0], meta[1], meta[2], meta[3]
    product[pl.ds(0, 2048), :] = dot(inverse[1], tile[0, 0]) * scale[1, 0]
    store_gram(meta, product, keep, send, 24)
    for s in range(STEPS):
        high, low = split(rhs[s])
        both = jnp.concatenate([high, low], axis=0)
        for dz in range(4):
            chunk = lax.rem(z + 4 - dz, 4) * 4 + x
            rows = inverse[s, pl.ds(pl.multiple_of(chunk * 128, 128), 128), :]
            base = (s * 4 + dz) * 128
            product[pl.ds(base, 128), :] = dot(jnp.concatenate([rows, rows], axis=1), both)
            for ey in range(4):
                row = base + lax.rem(y + ey, 4) * 32
                keep[ey, s * 4 + dz] = product[pl.ds(pl.multiple_of(row + u * 16, 16), 16), :]
                send[ey, s * 4 + dz] = product[pl.ds(pl.multiple_of(row + (1 - u) * 16, 16), 16), :]


def first_products(meta, scale, inverse, rhs, tiles):
    out = jax.ShapeDtypeStruct((4, 40, 16, 128), F32)
    return pl.pallas_call(
        first_kernel,
        grid_spec=pltpu.PrefetchScalarGridSpec(
            num_scalar_prefetch=2,
            grid=(1,),
            in_specs=[
                full((6, 2048, 256)),
                pl.BlockSpec((6, 256, 128), lambda i, m, s: (0, 0, m[3])),
                pl.BlockSpec((1, 1, 256, 128), lambda i, m, s: (1, 0, 0, 0)),
            ],
            out_specs=[full((4, 40, 16, 128))] * 2,
            scratch_shapes=[pltpu.VMEM((3072, 128), F32)],
        ),
        out_shape=[out, out],
        compiler_params=params(40),
        name="first_products",
    )(meta, scale, inverse, rhs, tiles)


def gram_kernel(meta, scale, blocks, inverse, tile, keep, send, product):
    i = pl.program_id(0)
    s, j = blocks[2 * i], blocks[2 * i + 1]
    product[...] = dot(inverse[0], tile[0, 0]) * scale[s, j]
    store_gram(meta, product, keep, send, 0)


def gram_products(meta, scale, inverse, tiles, pairs):
    count = len(pairs)
    out = jax.ShapeDtypeStruct((4, 16 * count, 16, 128), F32)
    block = pl.BlockSpec((4, 16, 16, 128), lambda i, m, s, b: (0, i, 0, 0))
    return pl.pallas_call(
        gram_kernel,
        grid_spec=pltpu.PrefetchScalarGridSpec(
            num_scalar_prefetch=3,
            grid=(count,),
            in_specs=[
                pl.BlockSpec((1, 2048, 256), lambda i, m, s, b: (b[2 * i], 0, 0)),
                pl.BlockSpec((1, 1, 256, 128), lambda i, m, s, b: (b[2 * i], b[2 * i + 1], 0, 0)),
            ],
            out_specs=[block, block],
            scratch_shapes=[pltpu.VMEM((2048, 128), F32)],
        ),
        out_shape=[out, out],
        compiler_params=params(24),
        name="gram_products",
    )(meta, scale, jnp.array([v for pair in pairs for v in pair], jnp.int32), inverse, tiles)


def step_kernel(count, meta, *refs):
    y, u = meta[1], meta[2]
    pieces, refs = refs[:4], refs[4:]
    older, refs = refs[: count - 1], refs[count - 1 :]
    gram, refs = refs[: 4 * count], refs[4 * count :]
    chunks, solved = refs[:4], refs[4]
    for ey in range(4):
        row = lax.rem(y + 4 - ey, 4) * 32
        for eu in range(2):
            at = pl.multiple_of(row + (u + eu - 2 * u * eu) * 16, 16)
            for dz in range(4):
                solved[dz, pl.ds(at, 16), :] = pieces[ey][eu, dz]
    total = jnp.zeros((256, 128), F32)
    for j in range(count):
        block = jnp.concatenate([ref[...].reshape(256, 128) for ref in gram[4 * j : 4 * j + 4]], axis=1)
        source = solved if j == count - 1 else older[j]
        total = total + dot3(block, source[...].reshape(512, 128))
    total = total.reshape(4, 4, 16, 128)
    for ex in range(4):
        chunks[ex][...] = total[ex]


def step(meta, pieces, older, gram):
    count = len(older) + 1
    specs = [full((2, 4, 16, 128))] * 4 + [full((4, 128, 128))] * len(older)
    operands = list(pieces) + list(older)
    for arrays, at in gram:
        for array in arrays:
            specs.append(pl.BlockSpec((16, 16, 128), functools.partial(lambda i, m, at: (at, 0, 0), at=at)))
            operands.append(array)
    return pl.pallas_call(
        functools.partial(step_kernel, count),
        grid_spec=pltpu.PrefetchScalarGridSpec(
            num_scalar_prefetch=1,
            grid=(1,),
            in_specs=specs,
            out_specs=[full((4, 16, 128))] * 4 + [full((4, 128, 128))],
        ),
        out_shape=[jax.ShapeDtypeStruct((4, 16, 128), F32)] * 4 + [jax.ShapeDtypeStruct((4, 128, 128), F32)],
        compiler_params=params(32),
        name="step",
    )(meta, *operands)


def last_kernel(meta, a, b, c, d, solved):
    y, u = meta[1], meta[2]
    for ey, piece in enumerate((a, b, c, d)):
        row = lax.rem(y + 4 - ey, 4) * 32
        for eu in range(2):
            at = pl.multiple_of(row + (u + eu - 2 * u * eu) * 16, 16)
            for dz in range(4):
                solved[dz, pl.ds(at, 16), :] = piece[eu, dz]


def last(meta, pieces):
    return pl.pallas_call(
        last_kernel,
        grid_spec=pltpu.PrefetchScalarGridSpec(
            num_scalar_prefetch=1, grid=(1,), in_specs=[full((2, 4, 16, 128))] * 4, out_specs=full((4, 128, 128))
        ),
        out_shape=jax.ShapeDtypeStruct((4, 128, 128), F32),
        name="last",
    )(meta, *pieces)


def sum_kernel(meta, a, b, c, d, start, out):
    z = meta[3]
    for dz in range(4):
        at = lax.rem(z + 4 - dz, 4)
        out[dz] = start[dz] - ((a[at] + b[at]) + (c[at] + d[at]))


def sum_x(meta, chunks, start, s):
    return pl.pallas_call(
        sum_kernel,
        grid_spec=pltpu.PrefetchScalarGridSpec(
            num_scalar_prefetch=1,
            grid=(1,),
            in_specs=[full((4, 16, 128))] * 4 + [pl.BlockSpec((4, 16, 128), lambda i, m: (s, 0, 0))],
            out_specs=full((4, 16, 128)),
        ),
        out_shape=jax.ShapeDtypeStruct((4, 16, 128), F32),
        name="sum_x",
    )(meta, *chunks, start)


def columns_kernel(count, meta, a, b, c, d, solved, both):
    z = meta[3]
    for k in range(count):
        for dz, piece in enumerate((a, b, c, d)):
            at = pl.multiple_of(lax.rem(z + 4 - dz, 4) * 128, 128)
            solved[k, :, pl.ds(at, 128)] = piece[k]
        high, low = split(solved[k])
        both[k, pl.ds(0, 128), :] = high
        both[k, pl.ds(128, 128), :] = low


def columns(meta, pieces):
    count = pieces[0].shape[0]
    return pl.pallas_call(
        functools.partial(columns_kernel, count),
        grid_spec=pltpu.PrefetchScalarGridSpec(
            num_scalar_prefetch=1,
            grid=(1,),
            in_specs=[full((count, 128, 128))] * 4,
            out_specs=[full((count, 128, 512)), full((count, 256, 512))],
        ),
        out_shape=[jax.ShapeDtypeStruct((count, 128, 512), F32), jax.ShapeDtypeStruct((count, 256, 512), BF16)],
        compiler_params=params(16),
        name="columns",
    )(meta, *pieces)


def trail_kernel(steps, blocks, scale, tile, both, *refs):
    i = pl.program_id(0)
    s = blocks[0] + i
    total = None if len(refs) == 1 else refs[0][0]
    for n, k in enumerate(steps):
        own = tile[0, n]
        part = dot(jnp.concatenate([own, own], axis=1), both[n]) * scale[s, k]
        total = part if total is None else total + part
    refs[-1][0] = total


def trail(first, scale, tiles, both, steps, total=None):
    count = 6 if len(steps) > 1 else 1
    k = steps[0] // count
    chunk = pl.BlockSpec((1, 256, 512), lambda i, b, s: (i, 0, 0))
    specs = [pl.BlockSpec((1, count, 256, 128), lambda i, b, s: (b[0] + i, k, 0, 0)), full(both.shape)]
    operands = [tiles, both]
    if total is not None:
        specs.append(chunk)
        operands.append(total)
    return pl.pallas_call(
        functools.partial(trail_kernel, steps),
        grid_spec=pltpu.PrefetchScalarGridSpec(num_scalar_prefetch=2, grid=(2,), in_specs=specs, out_specs=chunk),
        out_shape=jax.ShapeDtypeStruct((2, 256, 512), F32),
        compiler_params=params(24),
        name="trail",
    )(first, scale, *operands)


def sum_sub_kernel(me, a, b, c, d, *outs):
    for e in range(4):
        at = lax.rem(me[0] + e, 4)
        outs[e][...] = (a[at] + b[at]) + (c[at] + d[at])


def sum_sub(me, parts):
    return pl.pallas_call(
        sum_sub_kernel,
        grid_spec=pltpu.PrefetchScalarGridSpec(
            num_scalar_prefetch=1,
            grid=(1,),
            in_specs=[full((4, 128, 512))] * 4,
            out_specs=[full((128, 512))] * 4,
        ),
        out_shape=[jax.ShapeDtypeStruct((128, 512), F32)] * 4,
        compiler_params=params(24),
        name="sum_sub",
    )(me, *parts)


def finish_kernel(at, rhs, a, b, c, d, out):
    out[...] = rhs[0] - ((a[...] + b[...]) + (c[...] + d[...]))


def finish(at, rhs, parts):
    return pl.pallas_call(
        finish_kernel,
        grid_spec=pltpu.PrefetchScalarGridSpec(
            num_scalar_prefetch=1,
            grid=(1,),
            in_specs=[pl.BlockSpec((1, 128, 512), lambda i, at: (at[0], at[1], 0))] + [full((128, 512))] * 4,
            out_specs=full((128, 512)),
        ),
        out_shape=jax.ShapeDtypeStruct((128, 512), F32),
        name="finish",
    )(at, rhs, *parts)


def place_kernel(me, a, b, c, d, out):
    for e, piece in enumerate((a, b, c, d)):
        out[lax.rem(me[0] + 4 - e, 4)] = piece[...]


def place(me, parts):
    return pl.pallas_call(
        place_kernel,
        grid_spec=pltpu.PrefetchScalarGridSpec(
            num_scalar_prefetch=1, grid=(1,), in_specs=[full((128, 512))] * 4, out_specs=full((4, 128, 512))
        ),
        out_shape=jax.ShapeDtypeStruct((4, 128, 512), F32),
        name="place",
    )(me, *parts)


def on_device(rhs_blocks, factor_tiles, tile_scale, diag_inverse):
    row, column = lax.axis_index("prow"), lax.axis_index("pcol")
    y, u, z, x = row // 2, row % 2, column // 4, column % 4
    meta = jnp.stack([x, y, u, z]).astype(jnp.int32)
    tiles = jnp.transpose(factor_tiles, (0, 2, 1, 3))

    def shift(value, axis, d):
        if axis == "x":
            return lax.ppermute(value, "pcol", [(i, i // 4 * 4 + (i + d) % 4) for i in range(16)])
        if axis == "z":
            return lax.ppermute(value, "pcol", [(i, (i + 4 * d) % 16) for i in range(16)])
        if axis == "y":
            return lax.ppermute(value, "prow", [(i, (i + 2 * d) % 8) for i in range(8)])
        return lax.ppermute(value, "prow", [(i, i ^ 1) for i in range(8)])

    def exchange(values, axis):
        return [values[0]] + [shift(values[d], axis, d) for d in (1, 2, 3)]

    def spread(value, axis):
        return exchange([value] * 4, axis)

    def reduce_rows(keep, send):
        half = keep + shift(send, "core", 1)
        a, b, c, d = exchange([half[i] for i in range(4)], "y")
        return (a + b) + (c + d)

    def gather(piece):
        both = jnp.stack([piece, shift(piece, "core", 1)])
        return spread(both, "y")

    first = reduce_rows(*first_products(meta, tile_scale, diag_inverse, rhs_blocks, tiles))
    start = first[:24]
    grams = {(1, 0): (spread(first[24:], "z"), 0)}
    for pairs in PAIRS[1:]:
        total = reduce_rows(*gram_products(meta, tile_scale, diag_inverse, tiles, pairs))
        arrays = spread(total, "z")
        for n, pair in enumerate(pairs):
            grams[pair] = (arrays, n)

    solved = []
    piece = start[:4]
    for s in range(1, STEPS):
        *chunks, latest = step(meta, gather(piece), solved, [grams[s, j] for j in range(s)])
        solved.append(latest)
        piece = sum_x(meta, exchange(chunks, "x"), start, s)
    latest = last(meta, gather(piece))

    early = exchange([jnp.stack([v[-d % 4] for v in solved]) for d in range(4)], "z")
    solved_early, both_early = columns(meta, early)
    late = exchange([latest[-d % 4][None] for d in range(4)], "z")
    solved_late, both_late = columns(meta, late)

    halves = []
    for half, (one, two, me, other) in enumerate((("x", "z", x, z), ("z", "x", z, x))):
        base = 6 + 8 * half
        firsts = [(base + 2 * ((me + d) % 4)).astype(jnp.int32)[None] for d in range(4)]
        parts = [trail(at, tile_scale, tiles, both_early, range(5)) for at in firsts]
        parts = [trail(at, tile_scale, tiles, both_late, (5,), p) for at, p in zip(firsts, parts)]
        parts = [v.reshape(4, 128, 512) for v in exchange(parts, one)]
        subs = exchange(sum_sub(other.astype(jnp.int32)[None], parts), two)
        at = jnp.stack([base + 2 * me + other // 2, other % 2]).astype(jnp.int32)
        done = finish(at, rhs_blocks, subs)
        chunk = place(other.astype(jnp.int32)[None], spread(done, two)).reshape(2, 256, 512)
        halves.append((8 * half, me, spread(chunk, one)))
    trailing = jnp.zeros((16, 256, 512), F32)
    for base, me, chunks in halves:
        for d, chunk in enumerate(chunks):
            trailing = lax.dynamic_update_slice(trailing, chunk, (base + 2 * ((me - d) % 4), 0, 0))
    return jnp.concatenate([solved_early, solved_late]), trailing


def solution(mesh):
    in_specs = (P(None, "prow", None), P(None, "prow", None, "pcol"), P(), P(None, None, "prow"))
    out_specs = (P(None, "pcol", None), P(None, "prow", None))
    return jax.shard_map(
        on_device, mesh=mesh, in_specs=in_specs, out_specs=out_specs, check_vma=False
    )
```

```python
import functools

import jax
import jax.numpy as jnp
from jax import lax
from jax.experimental import pallas as pl
from jax.experimental.pallas import tpu as pltpu
from jax.sharding import PartitionSpec as P

F32 = jnp.float32
BF16 = jnp.bfloat16
STEPS = 6
V, H, S = (pl.BlockSpec(memory_space=m) for m in (pltpu.VMEM, pltpu.HBM, pltpu.SMEM))


def split(value):
    high = value.astype(BF16)
    return high, (value - high.astype(F32)).astype(BF16)


def dot(a, b):
    return jnp.dot(a, b, preferred_element_type=F32)


def call(kernel, name, mib, inputs, outputs, scratch=()):
    specs, operands = zip(*inputs)
    return pl.pallas_call(
        kernel,
        in_specs=specs,
        out_specs=[V] * len(outputs),
        out_shape=[jax.ShapeDtypeStruct(*o) for o in outputs],
        scratch_shapes=scratch,
        compiler_params=pltpu.CompilerParams(vmem_limit_bytes=mib << 20),
        name=name,
    )(*operands)


def fetch(pairs, sems):
    copies = [pltpu.make_async_copy(a, b, sems.at[i]) for i, (a, b) in enumerate(pairs)]
    for copy in copies:
        copy.start()
    return copies


def gram_kernel(blocks, s, meta, scale, inverse, rhs, tiles, _, __, keep, send, d_buf, r_buf, t_buf, product, sems):
    x, u, z = meta[0], meta[2], meta[3]
    group = pl.ds(pl.multiple_of(z * 128, 128), 128)
    copies = fetch(
        [(tiles.at[s, pl.ds(0, s)], t_buf)]
        + [(inverse.at[b], d_buf.at[i]) for i, b in enumerate(blocks)]
        + [(rhs.at[b, :, group], r_buf.at[i]) for i, b in enumerate(blocks)],
        sems,
    )
    for copy in copies:
        copy.wait()

    def store(slot, row, ey, at):
        row = row + ey * 32
        keep[ey, at] = product[slot, pl.ds(pl.multiple_of(row + u * 16, 16), 16), :]
        send[ey, at] = product[slot, pl.ds(pl.multiple_of(row + (1 - u) * 16, 16), 16), :]

    base = 4 * len(blocks)
    for j in range(s):
        slot = j % 2
        product[slot] = dot(d_buf[len(blocks) - 1], t_buf[j]) * scale[s, j]
        for zz in range(4):
            for ex in range(4):
                row = (zz * 4 + lax.rem(x + ex, 4)) * 128
                for ey in range(4):
                    store(slot, row, ey, base + 16 * j + ex * 4 + zz)
    slot = s % 2
    for i in range(len(blocks)):
        high, low = split(r_buf[i])
        both = jnp.concatenate([high, low], axis=0)
        for dz in range(4):
            chunk = lax.rem(z + 4 - dz, 4) * 4 + x
            rows = d_buf[i, pl.ds(pl.multiple_of(chunk * 128, 128), 128), :]
            row = (i * 4 + dz) * 128
            product[slot, pl.ds(row, 128), :] = dot(jnp.concatenate([rows, rows], axis=1), both)
            for ey in range(4):
                store(slot, row, ey, i * 4 + dz)


def gram(blocks, s, meta, scale, inverse, rhs, tiles, *after):
    out = ((4, 4 * len(blocks) + 16 * s, 16, 128), F32)
    n = len(blocks)
    return call(
        functools.partial(gram_kernel, blocks, s),
        "gram",
        58 if s == 1 else 32,
        [(S, meta), (S, scale), (H, inverse), (H, rhs), (H, tiles)] + [(H, a) for a in after],
        [out, out],
        [
            pltpu.VMEM((n, 2048, 256), BF16),
            pltpu.VMEM((n, 256, 128), F32),
            pltpu.VMEM((s, 256, 128), BF16),
            pltpu.VMEM((2, 2048, 128), F32),
            pltpu.SemaphoreType.DMA((1 + 2 * n,)),
        ],
    )


def step_kernel(count, meta, *refs):
    y, u, z = meta[1], meta[2], meta[3]
    pieces, refs = refs[:4], refs[4:]
    older, refs = refs[: count - 1], refs[count - 1 :]
    gathered = len(refs) == 8
    gram_refs, refs = refs[:-7], refs[-7:]
    chunks, solved, g_buf, sems = refs[:4], refs[4], refs[5], refs[6]
    sources = [gram_refs[0].at[lax.rem(z + 4 - d, 4)] if gathered else gram_refs[d] for d in range(4)]
    copies = fetch([(sources[d], g_buf.at[d]) for d in range(4)], sems)
    for ey in range(4):
        row = lax.rem(y + 4 - ey, 4) * 32
        for eu in range(2):
            at = pl.multiple_of(row + (u + eu - 2 * u * eu) * 16, 16)
            for dz in range(4):
                solved[dz, pl.ds(at, 16), :] = pieces[ey][eu, dz]
    for copy in copies:
        copy.wait()
    total = jnp.zeros((256, 128), F32)
    for j in range(count):
        block = jnp.concatenate([g_buf[d, pl.ds(16 * j, 16)].reshape(256, 128) for d in range(4)], axis=1)
        source = solved if j == count - 1 else older[j]
        a_high, a_low = split(block)
        b_high, b_low = split(source[...].reshape(512, 128))
        total = total + (dot(a_high, b_high) + (dot(a_high, b_low) + dot(a_low, b_high)))
    total = total.reshape(4, 4, 16, 128)
    for ex in range(4):
        for zz in range(4):
            chunks[ex][lax.rem(z + 4 - zz, 4)] = total[ex, zz]


def step(meta, pieces, older, pieces_z):
    count = len(older) + 1
    *chunks, solved = call(
        functools.partial(step_kernel, count),
        "step",
        24,
        [(S, meta)] + [(V, p) for p in pieces] + [(V, o) for o in older] + [(H, g) for g in pieces_z],
        [((4, 16, 128), F32)] * 4 + [((4, 128, 128), F32)],
        [pltpu.VMEM((4, 16 * count, 16, 128), F32), pltpu.SemaphoreType.DMA((4,))],
    )
    return chunks, solved


def early_kernel(meta, *refs):
    z = meta[3]
    own, others, solved, both = refs[:5], refs[5:8], refs[8], refs[9]
    for k in range(5):
        for d in range(4):
            at = pl.multiple_of(lax.rem(z + 4 - d, 4) * 128, 128)
            value = own[k][0] if d == 0 else others[d - 1][k]
            high, low = split(value)
            solved[k, :, pl.ds(at, 128)] = value
            both[k, pl.ds(0, 128), pl.ds(at, 128)] = high
            both[k, pl.ds(128, 128), pl.ds(at, 128)] = low


def early(meta, own, others):
    return call(
        early_kernel,
        "early",
        16,
        [(S, meta)] + [(V, o) for o in own] + [(V, o) for o in others],
        [((5, 128, 512), F32), ((5, 256, 512), BF16)],
    )


def late_kernel(meta, a, b, c, d, solved, both):
    y, u, z = meta[1], meta[2], meta[3]
    for ey, piece in enumerate((a, b, c, d)):
        row = lax.rem(y + 4 - ey, 4) * 32
        for eu in range(2):
            at = pl.multiple_of(row + (u + eu - 2 * u * eu) * 16, 16)
            low_at = pl.multiple_of(at + 128, 16)
            for dz in range(4):
                group = pl.ds(pl.multiple_of(lax.rem(z + 4 - dz, 4) * 128, 128), 128)
                value = piece[eu, dz]
                high, low = split(value)
                solved[0, pl.ds(at, 16), group] = value
                both[0, pl.ds(at, 16), group] = high
                both[0, pl.ds(low_at, 16), group] = low


def late(meta, pieces):
    return call(
        late_kernel,
        "late",
        8,
        [(S, meta)] + [(V, p) for p in pieces],
        [((1, 128, 512), F32), ((1, 256, 512), BF16)],
    )


def trail_kernel(count, first, scale, tiles, early_both, late_both, _, *refs):
    outs, t_buf, sems = refs[:count], refs[count], refs[count + 1]
    copies = fetch([(tiles.at[first[i]], t_buf.at[i]) for i in range(count)], sems)
    for i in range(count):
        copies[i].wait()
        total = None
        for k in range(STEPS):
            own = t_buf[i, k]
            value = early_both[k] if k < 5 else late_both[0]
            part = dot(jnp.concatenate([own, own], axis=1), value) * scale[first[i], k]
            total = part if total is None else total + part
        outs[i][...] = total


def trail(first, scale, tiles, early_both, late_both, after):
    count = first.shape[0]
    return call(
        functools.partial(trail_kernel, count),
        "trail",
        56,
        [(S, first), (S, scale), (H, tiles), (V, early_both), (V, late_both), (H, after)],
        [((256, 512), F32)] * count,
        [pltpu.VMEM((count, 6, 256, 128), BF16), pltpu.SemaphoreType.DMA((count,))],
    )


def sum_sub_kernel(me, a0, a1, b0, b1, c0, c1, *outs):
    for e in range(4):
        at = lax.rem(me[0] + e, 4)
        rows = pl.ds(pl.multiple_of(lax.rem(at, 2) * 128, 128), 128)

        @pl.when(at < 2)
        def _():
            outs[e][...] = a0[rows, :] + (b0[rows, :] + c0[rows, :])

        @pl.when(at >= 2)
        def _():
            outs[e][...] = a1[rows, :] + (b1[rows, :] + c1[rows, :])


def sum_sub(me, parts):
    return call(sum_sub_kernel, "sum_sub", 24, [(S, me)] + [(V, p) for p in parts], [((128, 512), F32)] * 4)


def finish_kernel(at, rhs, a, b, c, out, buf, sem):
    copy = pltpu.make_async_copy(rhs.at[at[0], pl.ds(pl.multiple_of(at[1] * 128, 128), 128)], buf, sem)
    copy.start()
    total = a[...] + (b[...] + c[...])
    copy.wait()
    out[...] = buf[...] - total


def finish(at, rhs, parts):
    return call(
        finish_kernel,
        "finish",
        56,
        [(S, at), (H, rhs)] + [(V, p) for p in parts],
        [((128, 512), F32)],
        [pltpu.VMEM((128, 512), F32), pltpu.SemaphoreType.DMA],
    )[0]


def place_kernel(me, own, back, ahead, low, high, out0, out1):
    def put(at, rows, value):
        start = pl.ds(pl.multiple_of(lax.rem(at, 2) * 128 + rows, 64), value.shape[0])

        @pl.when(at < 2)
        def _():
            out0[start, :] = value

        @pl.when(at >= 2)
        def _():
            out1[start, :] = value

    for e, ref in ((0, own), (3, back), (1, ahead)):
        put(lax.rem(me[0] + e, 4), 0, ref[...])
    put(lax.rem(me[0] + 2, 4), 0, low[...])
    put(lax.rem(me[0] + 2, 4), 64, high[...])


def place(me, parts):
    return call(place_kernel, "place", 16, [(S, me)] + [(V, p) for p in parts], [((256, 512), F32)] * 2)


def on_device(rhs_blocks, factor_tiles, tile_scale, diag_inverse):
    row, column = lax.axis_index("prow"), lax.axis_index("pcol")
    y, u, z, x = row // 2, row % 2, column // 4, column % 4
    meta = jnp.stack([x, y, u, z]).astype(jnp.int32)
    tiles = jnp.transpose(factor_tiles, (0, 2, 1, 3))

    def shift(value, axis, d):
        if axis == "x":
            return lax.ppermute(value, "pcol", [(i, i // 4 * 4 + (i + d) % 4) for i in range(16)])
        if axis == "z":
            return lax.ppermute(value, "pcol", [(i, (i + 4 * d) % 16) for i in range(16)])
        if axis == "y":
            return lax.ppermute(value, "prow", [(i, (i + 2 * d) % 8) for i in range(8)])
        return lax.ppermute(value, "prow", [(i, i ^ 1) for i in range(8)])

    def exchange(values, axis):
        return [values[0]] + [shift(values[d], axis, d) for d in (1, 2, 3)]

    def spread(value, axis):
        return exchange([value] * 4, axis)

    def reduce_rows(keep, send):
        half = keep + shift(send, "core", 1)
        groups = [[2 * i + core for i in range(4)] for core in range(2)]
        parts = lax.all_to_all(half, "prow", 0, 0, axis_index_groups=groups)
        return half, (parts[0] + parts[1]) + (parts[2] + parts[3])

    def gather_z(value):
        groups = [[4 * i + j for i in range(4)] for j in range(4)]
        return [lax.all_gather(value, "pcol", axis_index_groups=groups)]

    def gather(piece):
        both = jnp.stack([piece, shift(piece, "core", 1)])
        return both, spread(both, "y")

    start, grams = [], {}

    def make(s, *after):
        blocks = (0, 1) if s == 1 else (s,)
        half, total = reduce_rows(*gram(blocks, s, meta, tile_scale, diag_inverse, rhs_blocks, tiles, *after))
        start.extend(total[4 * i : 4 * i + 4] for i in range(len(blocks)))
        block = total[4 * len(blocks) :]
        grams[s] = spread(block, "z") if s < 3 else gather_z(block)
        return half

    half = make(2, make(1, meta, meta), meta)
    solved = []
    piece = start[0]
    for s in range(1, STEPS):
        both, pieces = gather(piece)
        if s == 1:
            half = make(3, half, both)
        chunks, latest = step(meta, pieces, solved, grams[s])
        if s < 3:
            half = make(s + 3, half, chunks[0])
        solved.append(latest)
        a, b, c, d = exchange(chunks, "x")
        piece = start[s] - ((a + b) + (c + d))

    others = exchange([jnp.stack([v[-d % 4] for v in solved]) for d in range(4)], "z")[1:]
    solved_early, both_early = early(meta, solved, others)
    piece = jnp.stack(exchange([piece[-d % 4] for d in range(4)], "z"))
    solved_late, both_late = late(meta, gather(piece)[1])

    axes = (("x", "z", x, z, 6), ("z", "x", z, x, 14))

    def chunks_of(offsets, after):
        first = jnp.stack([base + 2 * ((me + d) % 4) + i for d in offsets for _, _, me, _, base in axes for i in range(2)])
        return trail(first.astype(jnp.int32), tile_scale, tiles, both_early, both_late, after)

    def ring(values):
        return [(shift(up, axis, 1), shift(down, axis, 3)) for axis, up, down in values]

    one, two = [a[0] for a in axes], [a[1] for a in axes]
    far = chunks_of((2,), meta)
    moved = ring([(one[h], far[2 * h], far[2 * h + 1]) for h in range(2)])
    near = chunks_of((1, 3), far[0])
    own = chunks_of((0,), near[0])
    ups = [jnp.stack([near[2 * h] + moved[h][0], near[2 * h + 1]]) for h in range(2)]
    downs = [jnp.stack([near[4 + 2 * h], near[5 + 2 * h] + moved[h][1]]) for h in range(2)]
    moved = ring([(one[h], ups[h], downs[h]) for h in range(2)])
    subs = []
    for h in range(2):
        other = axes[h][3].astype(jnp.int32)[None]
        below, above = moved[h]
        subs.append(sum_sub(other, (own[2 * h], own[2 * h + 1], below[0], below[1], above[0], above[1])))
    moved = ring([(two[h], subs[h][2][:64], subs[h][2][64:]) for h in range(2)])
    ups = [subs[h][1].at[:64].add(moved[h][0]) for h in range(2)]
    downs = [subs[h][3].at[64:].add(moved[h][1]) for h in range(2)]
    moved = ring([(two[h], ups[h], downs[h]) for h in range(2)])
    done = []
    for h, (_, _, me, other, base) in enumerate(axes):
        at = jnp.stack([base + 2 * me + other // 2, other % 2]).astype(jnp.int32)
        done.append(finish(at, rhs_blocks, (subs[h][0],) + moved[h]))
    near = ring([(two[h], done[h], done[h]) for h in range(2)])
    far = ring([(two[h], near[h][0][:64], near[h][1][64:]) for h in range(2)])
    own = []
    for h in range(2):
        other = axes[h][3].astype(jnp.int32)[None]
        own.append(jnp.stack(place(other, (done[h],) + near[h] + far[h])))
    near = ring([(one[h], own[h], own[h]) for h in range(2)])
    far = ring([(one[h], near[h][0][0], near[h][1][1]) for h in range(2)])
    trailing = jnp.zeros((16, 256, 512), F32)
    for h, (_, _, me, _, base) in enumerate(axes):
        base = base - 6
        far_chunk = base + 2 * ((me + 2) % 4)
        trailing = lax.dynamic_update_slice(trailing, own[h], (base + 2 * me, 0, 0))
        trailing = lax.dynamic_update_slice(trailing, near[h][0], (base + 2 * ((me + 3) % 4), 0, 0))
        trailing = lax.dynamic_update_slice(trailing, near[h][1], (base + 2 * ((me + 1) % 4), 0, 0))
        trailing = lax.dynamic_update_slice(trailing, far[h][0][None], (far_chunk, 0, 0))
        trailing = lax.dynamic_update_slice(trailing, far[h][1][None], (far_chunk + 1, 0, 0))
    return jnp.concatenate([solved_early, solved_late]), trailing


def solution(mesh):
    in_specs = (P(None, "prow", None), P(None, "prow", None, "pcol"), P(), P(None, None, "prow"))
    out_specs = (P(None, "pcol", None), P(None, "prow", None))
    return jax.shard_map(
        on_device, mesh=mesh, in_specs=in_specs, out_specs=out_specs, check_vma=False
    )
```

```python
import functools

import jax
import jax.numpy as jnp
from jax import lax
from jax.experimental import pallas as pl
from jax.experimental.pallas import tpu as pltpu
from jax.sharding import PartitionSpec as P

F32 = jnp.float32
BF16 = jnp.bfloat16
STEPS = 6
V, H, S = (pl.BlockSpec(memory_space=m) for m in (pltpu.VMEM, pltpu.HBM, pltpu.SMEM))


def split(value):
    high = value.astype(BF16)
    return high, (value - high.astype(F32)).astype(BF16)


def dot(a, b):
    return jnp.dot(a, b, preferred_element_type=F32)


def call(kernel, name, mib, inputs, outputs, scratch=()):
    specs, operands = zip(*inputs)
    return pl.pallas_call(
        kernel,
        in_specs=specs,
        out_specs=[V] * len(outputs),
        out_shape=[jax.ShapeDtypeStruct(*o) for o in outputs],
        scratch_shapes=scratch,
        compiler_params=pltpu.CompilerParams(vmem_limit_bytes=mib << 20),
        name=name,
    )(*operands)


def fetch(pairs, sems):
    copies = [pltpu.make_async_copy(a, b, sems.at[i]) for i, (a, b) in enumerate(pairs)]
    for copy in copies:
        copy.start()
    return copies


def gram_kernel(rows, extra, whole, meta, scale, inverse, rhs, tiles, *refs):
    outs = refs[-6:-5] if whole else refs[-7:-5]
    d_buf, r_buf, t_buf, product, sems = refs[-5:]
    x, y, u, z = meta[0], meta[1], meta[2], meta[3]
    blocks = extra + rows
    group = pl.ds(pl.multiple_of(z * 128, 128), 128)
    copies = []
    sem = 0
    for i, b in enumerate(blocks):
        copies.append(fetch([(inverse.at[b], d_buf.at[i]), (rhs.at[b, :, group], r_buf.at[i])], sems.at[pl.ds(sem, 2)]))
        sem += 2
    base = 0
    for s in rows:
        copies[len(extra) + rows.index(s)] += fetch(
            [(tiles.at[s, pl.ds(0, s)], t_buf.at[pl.ds(base, s)])], sems.at[pl.ds(sem, 1)]
        )
        sem += 1
        base += s

    def store(slot, row, at):
        for yy in range(4):
            if whole:
                for core in range(2):
                    outs[0][2 * yy + core, at] = product[slot, pl.ds(pl.multiple_of(row + yy * 32 + core * 16, 16), 16), :]
            else:
                ey = lax.rem(yy + 4 - y, 4) if extra else yy
                start = row + yy * 32
                outs[0][ey, at] = product[slot, pl.ds(pl.multiple_of(start + u * 16, 16), 16), :]
                outs[1][ey, at] = product[slot, pl.ds(pl.multiple_of(start + (1 - u) * 16, 16), 16), :]

    turn = 0
    base = 0
    unit = 4 * len(blocks)
    for i, b in enumerate(blocks):
        for copy in copies[i]:
            copy.wait()
        high, low = split(r_buf[i])
        both = jnp.concatenate([high, low], axis=0)
        slot = turn % 2
        turn += 1
        for dz in range(4):
            chunk = lax.rem(z + 4 - dz, 4) * 4 + x
            part = d_buf[i, pl.ds(pl.multiple_of(chunk * 128, 128), 128), :]
            product[slot, pl.ds(dz * 128, 128), :] = dot(jnp.concatenate([part, part], axis=1), both)
            store(slot, dz * 128, i * 4 + dz)
        if b not in rows:
            continue
        for j in range(b):
            slot = turn % 2
            turn += 1
            product[slot] = dot(d_buf[i], t_buf[base]) * scale[b, j]
            base += 1
            for zz in range(4):
                for ex in range(4):
                    store(slot, (zz * 4 + lax.rem(x + ex, 4)) * 128, unit + ex * 4 + zz)
            unit += 16


def gram(rows, extra, whole, meta, scale, inverse, rhs, tiles, *after):
    n = len(extra) + len(rows)
    units = 4 * n + 16 * sum(rows)
    outputs = [((8, units, 16, 128), F32)] if whole else [((4, units, 16, 128), F32)] * 2
    return call(
        functools.partial(gram_kernel, rows, extra, whole),
        "gram",
        58,
        [(S, meta), (S, scale), (H, inverse), (H, rhs), (H, tiles)] + [(H, a) for a in after],
        outputs,
        [
            pltpu.VMEM((n, 2048, 256), BF16),
            pltpu.VMEM((n, 256, 128), F32),
            pltpu.VMEM((sum(rows), 256, 128), BF16),
            pltpu.VMEM((2, 2048, 128), F32),
            pltpu.SemaphoreType.DMA((2 * n + len(rows),)),
        ],
    )


def step_kernel(count, meta, *refs):
    y, u, z = meta[1], meta[2], meta[3]
    pieces, refs = refs[:4], refs[4:]
    older, refs = refs[: count - 1], refs[count - 1 :]
    gram_refs, refs = refs[:-7], refs[-7:]
    chunks, solved, g_buf, sems = refs[:4], refs[4], refs[5], refs[6]
    targets = [g_buf.at[d] for d in (0, 1, 3, 2)]
    if len(gram_refs) == 5:
        targets[3:] = [g_buf.at[2, pl.ds(0, 8 * count)], g_buf.at[2, pl.ds(8 * count, 8 * count)]]
    copies = fetch(list(zip(gram_refs, targets)), sems)
    for ey in range(4):
        row = lax.rem(y + 4 - ey, 4) * 32
        for eu in range(2):
            at = pl.multiple_of(row + (u + eu - 2 * u * eu) * 16, 16)
            for dz in range(4):
                solved[dz, pl.ds(at, 16), :] = pieces[ey][eu, dz]
    for copy in copies:
        copy.wait()
    total = jnp.zeros((256, 128), F32)
    for j in range(count):
        block = jnp.concatenate([g_buf[d, pl.ds(16 * j, 16)].reshape(256, 128) for d in range(4)], axis=1)
        source = solved if j == count - 1 else older[j]
        a_high, a_low = split(block)
        b_high, b_low = split(source[...].reshape(512, 128))
        total = total + (dot(a_high, b_high) + (dot(a_high, b_low) + dot(a_low, b_high)))
    total = total.reshape(4, 4, 16, 128)
    for ex in range(4):
        for zz in range(4):
            chunks[ex][lax.rem(z + 4 - zz, 4)] = total[ex, zz]


def step(meta, pieces, older, pieces_z):
    count = len(older) + 1
    *chunks, solved = call(
        functools.partial(step_kernel, count),
        "step",
        24,
        [(S, meta)] + [(V, p) for p in pieces] + [(V, o) for o in older] + [(H, g) for g in pieces_z],
        [((4, 16, 128), F32)] * 4 + [((4, 128, 128), F32)],
        [pltpu.VMEM((4, 16 * count, 16, 128), F32), pltpu.SemaphoreType.DMA((5,))],
    )
    return chunks, solved


def early_kernel(meta, *refs):
    z = meta[3]
    own, others, solved, both = refs[:5], refs[5:8], refs[8], refs[9]
    for k in range(5):
        for d in range(4):
            at = pl.multiple_of(lax.rem(z + 4 - d, 4) * 128, 128)
            value = own[k][0] if d == 0 else others[d - 1][k]
            high, low = split(value)
            solved[k, :, pl.ds(at, 128)] = value
            both[k, pl.ds(0, 128), pl.ds(at, 128)] = high
            both[k, pl.ds(128, 128), pl.ds(at, 128)] = low


def early(meta, own, others):
    return call(
        early_kernel,
        "early",
        16,
        [(S, meta)] + [(V, o) for o in own] + [(V, o) for o in others],
        [((5, 128, 512), F32), ((5, 256, 512), BF16)],
    )


def late_kernel(meta, a, b, c, d, solved, both):
    y, u, z = meta[1], meta[2], meta[3]
    for ey, piece in enumerate((a, b, c, d)):
        row = lax.rem(y + 4 - ey, 4) * 32
        for eu in range(2):
            at = pl.multiple_of(row + (u + eu - 2 * u * eu) * 16, 16)
            low_at = pl.multiple_of(at + 128, 16)
            for dz in range(4):
                group = pl.ds(pl.multiple_of(lax.rem(z + 4 - dz, 4) * 128, 128), 128)
                value = piece[eu, dz]
                high, low = split(value)
                solved[0, pl.ds(at, 16), group] = value
                both[0, pl.ds(at, 16), group] = high
                both[0, pl.ds(low_at, 16), group] = low


def late(meta, pieces):
    return call(
        late_kernel,
        "late",
        8,
        [(S, meta)] + [(V, p) for p in pieces],
        [((1, 128, 512), F32), ((1, 256, 512), BF16)],
    )


def trail_kernel(first, scale, tiles, early_both, late_both, *refs):
    outs, t_buf, sems = refs[:-2], refs[-2], refs[-1]
    count = sum(out.shape[0] for out in outs)
    copies = fetch([(tiles.at[first[i]], t_buf.at[i]) for i in range(count)], sems)
    i = 0
    for out in outs:
        for block in range(out.shape[0]):
            copies[i].wait()
            total = None
            for k in range(STEPS):
                own = t_buf[i, k]
                value = early_both[k] if k < 5 else late_both[0]
                part = dot(jnp.concatenate([own, own], axis=1), value) * scale[first[i], k]
                total = part if total is None else total + part
            out[block] = total
            i += 1


def trail_first_kernel(first, scale, tiles, early_both, late_both, *refs):
    trail_kernel(first, scale, tiles, early_both, late_both, *refs)


def trail_rest_kernel(first, scale, tiles, early_both, late_both, _, *refs):
    trail_kernel(first, scale, tiles, early_both, late_both, *refs)


def trail(first, scale, tiles, early_both, late_both, blocks, *after):
    count = first.shape[0]
    return call(
        trail_rest_kernel if after else trail_first_kernel,
        "trail",
        24 if after else 58,
        [(S, first), (S, scale), (H, tiles), (V, early_both), (V, late_both)] + [(H, a) for a in after],
        [((blocks, 256, 512), F32)] * (count // blocks),
        [pltpu.VMEM((count, 6, 256, 128), BF16), pltpu.SemaphoreType.DMA((count,))],
    )


def sum_sub_kernel(where, *refs):
    for h in range(2):
        a, b, c = refs[3 * h : 3 * h + 3]
        outs = refs[6 + 5 * h : 11 + 5 * h]

        def rows(e):
            at = lax.rem(where[h] + e, 4)
            return a[at] + (b[at] + c[at])

        outs[0][...] = rows(0)
        outs[1][...] = rows(1)
        outs[2][...] = rows(3)
        far = rows(2)
        outs[3][...] = far[:64]
        outs[4][...] = far[64:]


def sum_sub(where, parts):
    outputs = [((128, 512), F32)] * 3 + [((64, 512), F32)] * 2
    return call(sum_sub_kernel, "sum_sub", 32, [(S, where)] + [(V, p) for p in parts], outputs * 2)


def finish_kernel(at, rhs, *refs):
    parts, outs, buf, sems = refs[:6], refs[6:8], refs[8], refs[9]
    copies = fetch(
        [(rhs.at[at[2 * h], pl.ds(pl.multiple_of(at[2 * h + 1] * 128, 128), 128)], buf.at[h]) for h in range(2)], sems
    )
    for h in range(2):
        a, b, c = parts[3 * h : 3 * h + 3]
        copies[h].wait()
        outs[h][...] = buf[h] - (a[...] + (b[...] + c[...]))


def finish(at, rhs, parts):
    return call(
        finish_kernel,
        "finish",
        54,
        [(S, at), (H, rhs)] + [(V, p) for p in parts],
        [((128, 512), F32)] * 2,
        [pltpu.VMEM((2, 128, 512), F32), pltpu.SemaphoreType.DMA((2,))],
    )


def place_kernel(where, *refs):
    for h in range(2):
        own, back, ahead, low, high = refs[5 * h : 5 * h + 5]
        out = refs[10 + h]
        for e, ref in ((0, own), (3, back), (1, ahead)):
            out[lax.rem(where[h] + e, 4)] = ref[...]
        far = lax.rem(where[h] + 2, 4)
        out[far, pl.ds(0, 64), :] = low[...]
        out[far, pl.ds(64, 64), :] = high[...]


def place(where, parts):
    return call(place_kernel, "place", 16, [(S, where)] + [(V, p) for p in parts], [((4, 128, 512), F32)] * 2)


def write_kernel(starts, *refs):
    count = (len(refs) - 2) if len(refs) % 2 == 0 else (len(refs) - 3)
    values, out, sems = refs[:count], refs[-2], refs[-1]
    copies = fetch([(value, out.at[pl.ds(starts[i], value.shape[0])]) for i, value in enumerate(values)], sems)
    for copy in copies:
        copy.wait()


def write(starts, values, out=None):
    operands = [starts] + list(values) + ([] if out is None else [out])
    return pl.pallas_call(
        write_kernel,
        in_specs=[S] + [H] * (len(operands) - 1),
        out_specs=H,
        out_shape=jax.ShapeDtypeStruct((16, 256, 512), F32),
        scratch_shapes=[pltpu.SemaphoreType.DMA((len(values),))],
        input_output_aliases={} if out is None else {len(operands) - 1: 0},
        name="write",
    )(*operands)


def on_device(rhs_blocks, factor_tiles, tile_scale, diag_inverse):
    row, column = lax.axis_index("prow"), lax.axis_index("pcol")
    y, u, z, x = row // 2, row % 2, column // 4, column % 4
    meta = jnp.stack([x, y, u, z]).astype(jnp.int32)
    tiles = jnp.transpose(factor_tiles, (0, 2, 1, 3))

    def shift(value, axis, d):
        if axis == "x":
            return lax.ppermute(value, "pcol", [(i, i // 4 * 4 + (i + d) % 4) for i in range(16)])
        if axis == "z":
            return lax.ppermute(value, "pcol", [(i, (i + 4 * d) % 16) for i in range(16)])
        if axis == "y":
            return lax.ppermute(value, "prow", [(i, (i + 2 * d) % 8) for i in range(8)])
        return lax.ppermute(value, "prow", [(i, i ^ 1) for i in range(8)])

    def exchange(values, axis):
        return [values[0]] + [shift(values[d], axis, d) for d in (1, 2, 3)]

    def spread(value, axis):
        return exchange([value] * 4, axis)

    def ring(values):
        return [(shift(up, axis, 1), shift(down, axis, 3)) for axis, up, down in values]

    def ring_z(value):
        half = value.shape[0] // 2
        near = ring([("z", value, value)])[0]
        far = ring([("z", near[0][:half], near[1][half:])])[0]
        return (value,) + near + far

    def make(rows, extra, whole, *after):
        return gram(rows, extra, whole, meta, tile_scale, diag_inverse, rhs_blocks, tiles, *after)

    def gather(piece):
        both = jnp.stack([piece, shift(piece, "core", 1)])
        return both, spread(both, "y")

    keep, send = make((1,), (0,), False)
    half = keep + shift(send, "core", 1)
    a, b, c, d = exchange([half[i] for i in range(4)], "y")
    total = (a + b) + (c + d)
    start = {0: total[:4], 1: total[4:8]}
    a, b, c, d = spread(total[8:], "z")
    grams = {1: (a, b, d, c)}

    keep, send = make((2,), (), False, keep)
    half_2 = keep + shift(send, "core", 1)
    groups = [[2 * i + core for i in range(4)] for core in range(2)]
    parts = lax.all_to_all(half_2, "prow", 0, 0, axis_index_groups=groups)
    total = (parts[0] + parts[1]) + (parts[2] + parts[3])
    start[2] = total[:4]
    grams[2] = ring_z(total[4:])

    total = lax.psum_scatter(make((3, 4), (), True, half, keep)[0], "prow")
    start[3], start[4] = total[:4], total[4:8]
    grams[3], grams[4] = ring_z(total[8:56]), ring_z(total[56:])

    solved = []
    piece = start[0]
    for s in range(1, STEPS):
        both, pieces = gather(piece)
        if s == 1:
            total = lax.psum_scatter(make((5,), (), True, both)[0], "prow")
            start[5] = total[:4]
            grams[5] = ring_z(total[4:])
        chunks, latest = step(meta, pieces, solved, grams[s])
        solved.append(latest)
        a, b, c, d = exchange(chunks, "x")
        piece = start[s] - ((a + b) + (c + d))

    others = exchange([jnp.stack([v[-d % 4] for v in solved]) for d in range(4)], "z")[1:]
    solved_early, both_early = early(meta, solved, others)
    piece = jnp.stack(exchange([piece[-d % 4] for d in range(4)], "z"))
    solved_late, both_late = late(meta, gather(piece)[1])

    axes = (("x", "z", x, z, 6), ("z", "x", z, x, 14))
    one, two = [a[0] for a in axes], [a[1] for a in axes]
    where = jnp.stack([a[3] for a in axes]).astype(jnp.int32)

    def chunks_of(offsets, blocks, *after):
        first = jnp.stack([base + 2 * ((me + d) % 4) + i for d in offsets for _, _, me, _, base in axes for i in range(2)])
        return trail(first.astype(jnp.int32), tile_scale, tiles, both_early, both_late, blocks, *after)

    far = chunks_of((2,), 1)
    near = chunks_of((1, 3, 0), 2, far[0])
    moved = ring([(one[h], far[2 * h], far[2 * h + 1]) for h in range(2)])
    ups = [near[h].at[:1].add(moved[h][0]) for h in range(2)]
    downs = [near[2 + h].at[1:].add(moved[h][1]) for h in range(2)]
    moved = ring([(one[h], ups[h], downs[h]) for h in range(2)])
    terms = [v.reshape(4, 128, 512) for h in range(2) for v in (near[4 + h],) + moved[h]]
    subs = sum_sub(where, terms)
    subs = [subs[:5], subs[5:]]
    moved = ring([(two[h], subs[h][3], subs[h][4]) for h in range(2)])
    ups = [subs[h][1].at[:64].add(moved[h][0]) for h in range(2)]
    downs = [subs[h][2].at[64:].add(moved[h][1]) for h in range(2)]
    moved = ring([(two[h], ups[h], downs[h]) for h in range(2)])
    at = jnp.stack([v for _, _, me, other, base in axes for v in (base + 2 * me + other // 2, other % 2)])
    done = finish(at.astype(jnp.int32), rhs_blocks, [v for h in range(2) for v in (subs[h][0],) + moved[h]])
    near = ring([(two[h], done[h], done[h]) for h in range(2)])
    far = ring([(two[h], near[h][0][:64], near[h][1][64:]) for h in range(2)])
    own = place(where, [v for h in range(2) for v in (done[h],) + near[h] + far[h]])
    own = [v.reshape(2, 256, 512) for v in own]
    near = ring([(one[h], own[h], own[h]) for h in range(2)])
    far = ring([(one[h], near[h][0][:1], near[h][1][1:]) for h in range(2)])
    at = jnp.stack([base - 6 + 2 * ((me + d) % 4) for _, _, me, _, base in axes for d in (0, 3, 1)])
    trailing = write(at.astype(jnp.int32), [v for h in range(2) for v in (own[h],) + near[h]])
    at = jnp.stack([base - 6 + 2 * ((me + 2) % 4) + i for _, _, me, _, base in axes for i in range(2)])
    trailing = write(at.astype(jnp.int32), [v for h in range(2) for v in far[h]], trailing)
    return jnp.concatenate([solved_early, solved_late]), trailing


def solution(mesh):
    in_specs = (P(None, "prow", None), P(None, "prow", None, "pcol"), P(), P(None, None, "prow"))
    out_specs = (P(None, "pcol", None), P(None, "prow", None))
    return jax.shard_map(
        on_device, mesh=mesh, in_specs=in_specs, out_specs=out_specs, check_vma=False
    )
```

```python
import functools

import jax
import jax.numpy as jnp
from jax import lax
from jax.experimental import pallas as pl
from jax.experimental.pallas import tpu as pltpu
from jax.sharding import PartitionSpec as P

F32 = jnp.float32
BF16 = jnp.bfloat16
STEPS = 6
RING = 192
V, H, S = (pl.BlockSpec(memory_space=m) for m in (pltpu.VMEM, pltpu.HBM, pltpu.SMEM))


def split(value):
    high = value.astype(BF16)
    return high, (value - high.astype(F32)).astype(BF16)


def dot(a, b):
    return jnp.dot(a, b, preferred_element_type=F32)


def call(kernel, name, mib, inputs, outputs, scratch=(), blocks=0):
    specs, operands = zip(*inputs)
    return pl.pallas_call(
        kernel,
        in_specs=specs,
        out_specs=[V] * len(outputs),
        out_shape=[jax.ShapeDtypeStruct(*o) for o in outputs],
        scratch_shapes=scratch,
        compiler_params=pltpu.CompilerParams(vmem_limit_bytes=mib << 20),
        cost_estimate=pl.CostEstimate(flops=0, bytes_accessed=blocks << 22, transcendentals=0) if blocks else None,
        name=name,
    )(*operands)


def fetch(pairs, sems):
    copies = [pltpu.make_async_copy(a, b, sems.at[i]) for i, (a, b) in enumerate(pairs)]
    for copy in copies:
        copy.start()
    return copies


def gram_kernel(rows, extra, whole, meta, scale, inverse, rhs, tiles, *refs):
    outs = refs[-6:-5] if whole else refs[-7:-5]
    d_buf, r_buf, t_buf, product, sems = refs[-5:]
    x, y, u, z = meta[0], meta[1], meta[2], meta[3]
    blocks = extra + rows
    group = pl.ds(pl.multiple_of(z * 128, 128), 128)
    copies = []
    sem = 0
    for i, b in enumerate(blocks):
        copies.append(fetch([(inverse.at[b], d_buf.at[i]), (rhs.at[b, :, group], r_buf.at[i])], sems.at[pl.ds(sem, 2)]))
        sem += 2
    base = 0
    for s in rows:
        copies[len(extra) + rows.index(s)] += fetch(
            [(tiles.at[s, pl.ds(0, s)], t_buf.at[pl.ds(base, s)])], sems.at[pl.ds(sem, 1)]
        )
        sem += 1
        base += s

    def store(slot, row, at):
        for yy in range(4):
            if whole:
                for core in range(2):
                    outs[0][2 * yy + core, at] = product[slot, pl.ds(pl.multiple_of(row + yy * 32 + core * 16, 16), 16), :]
            else:
                ey = lax.rem(yy + 4 - y, 4) if extra else yy
                start = row + yy * 32
                outs[0][ey, at] = product[slot, pl.ds(pl.multiple_of(start + u * 16, 16), 16), :]
                outs[1][ey, at] = product[slot, pl.ds(pl.multiple_of(start + (1 - u) * 16, 16), 16), :]

    turn = 0
    base = 0
    unit = 4 * len(blocks)
    for i, b in enumerate(blocks):
        for copy in copies[i]:
            copy.wait()
        high, low = split(r_buf[i])
        both = jnp.concatenate([high, low], axis=0)
        slot = turn % 2
        turn += 1
        for dz in range(4):
            chunk = lax.rem(z + 4 - dz, 4) * 4 + x
            part = d_buf[i, pl.ds(pl.multiple_of(chunk * 128, 128), 128), :]
            product[slot, pl.ds(dz * 128, 128), :] = dot(jnp.concatenate([part, part], axis=1), both)
            store(slot, dz * 128, i * 4 + dz)
        if b not in rows:
            continue
        for j in range(b):
            slot = turn % 2
            turn += 1
            product[slot] = dot(d_buf[i], t_buf[base]) * scale[b, j]
            base += 1
            for zz in range(4):
                for ex in range(4):
                    store(slot, (zz * 4 + lax.rem(x + ex, 4)) * 128, unit + ex * 4 + zz)
            unit += 16


def gram(rows, extra, whole, meta, scale, inverse, rhs, tiles, *after):
    n = len(extra) + len(rows)
    units = 4 * n + 16 * sum(rows)
    outputs = [((8, units, 16, 128), F32)] if whole else [((4, units, 16, 128), F32)] * 2
    return call(
        functools.partial(gram_kernel, rows, extra, whole),
        "gram",
        58,
        [(S, meta), (S, scale), (H, inverse), (H, rhs), (H, tiles)] + [(H, a) for a in after],
        outputs,
        [
            pltpu.VMEM((n, 2048, 256), BF16),
            pltpu.VMEM((n, 256, 128), F32),
            pltpu.VMEM((sum(rows), 256, 128), BF16),
            pltpu.VMEM((2, 2048, 128), F32),
            pltpu.SemaphoreType.DMA((2 * n + len(rows),)),
        ],
        sum(rows) + 2,
    )


def step_kernel(count, meta, *refs):
    y, u, z = meta[1], meta[2], meta[3]
    pieces, refs = refs[:4], refs[4:]
    older, refs = refs[: count - 1], refs[count - 1 :]
    gram_refs, refs = refs[:-7], refs[-7:]
    chunks, solved, g_buf, sems = refs[:4], refs[4], refs[5], refs[6]
    targets = [g_buf.at[d] for d in (0, 1, 3, 2)]
    if len(gram_refs) == 5:
        targets[3:] = [g_buf.at[2, pl.ds(0, 8 * count)], g_buf.at[2, pl.ds(8 * count, 8 * count)]]
    copies = fetch(list(zip(gram_refs, targets)), sems)
    for ey in range(4):
        row = lax.rem(y + 4 - ey, 4) * 32
        for eu in range(2):
            at = pl.multiple_of(row + (u + eu - 2 * u * eu) * 16, 16)
            for dz in range(4):
                solved[dz, pl.ds(at, 16), :] = pieces[ey][eu, dz]
    for copy in copies:
        copy.wait()
    total = jnp.zeros((256, 128), F32)
    for j in range(count):
        block = jnp.concatenate([g_buf[d, pl.ds(16 * j, 16)].reshape(256, 128) for d in range(4)], axis=1)
        source = solved if j == count - 1 else older[j]
        a_high, a_low = split(block)
        b_high, b_low = split(source[...].reshape(512, 128))
        total = total + (dot(a_high, b_high) + (dot(a_high, b_low) + dot(a_low, b_high)))
    total = total.reshape(4, 4, 16, 128)
    for ex in range(4):
        for zz in range(4):
            chunks[ex][lax.rem(z + 4 - zz, 4)] = total[ex, zz]


def step(meta, pieces, older, pieces_z):
    count = len(older) + 1
    *chunks, solved = call(
        functools.partial(step_kernel, count),
        "step",
        24,
        [(S, meta)] + [(V, p) for p in pieces] + [(V, o) for o in older] + [(H, g) for g in pieces_z],
        [((4, 16, 128), F32)] * 4 + [((4, 128, 128), F32)],
        [pltpu.VMEM((4, 16 * count, 16, 128), F32), pltpu.SemaphoreType.DMA((5,))],
    )
    return chunks, solved


def early_kernel(meta, *refs):
    z = meta[3]
    own, others, solved, both = refs[:5], refs[5:8], refs[8], refs[9]
    for k in range(5):
        for d in range(4):
            at = pl.multiple_of(lax.rem(z + 4 - d, 4) * 128, 128)
            value = own[k][0] if d == 0 else others[d - 1][k]
            high, low = split(value)
            solved[k, :, pl.ds(at, 128)] = value
            both[k, pl.ds(0, 128), pl.ds(at, 128)] = high
            both[k, pl.ds(128, 128), pl.ds(at, 128)] = low


def early(meta, own, others):
    return call(
        early_kernel,
        "early",
        16,
        [(S, meta)] + [(V, o) for o in own] + [(V, o) for o in others],
        [((5, 128, 512), F32), ((5, 256, 512), BF16)],
    )


def late_kernel(meta, a, b, c, d, _, solved, both):
    y, u, z = meta[1], meta[2], meta[3]
    for ey, piece in enumerate((a, b, c, d)):
        row = lax.rem(y + 4 - ey, 4) * 32
        for eu in range(2):
            at = pl.multiple_of(row + (u + eu - 2 * u * eu) * 16, 16)
            low_at = pl.multiple_of(at + 128, 16)
            for dz in range(4):
                group = pl.ds(pl.multiple_of(lax.rem(z + 4 - dz, 4) * 128, 128), 128)
                value = piece[eu, dz]
                high, low = split(value)
                solved[0, pl.ds(at, 16), group] = value
                both[0, pl.ds(at, 16), group] = high
                both[0, pl.ds(low_at, 16), group] = low


def late(meta, pieces, after):
    return call(
        late_kernel,
        "late",
        8,
        [(S, meta)] + [(V, p) for p in pieces] + [(H, after)],
        [((1, 128, 512), F32), ((1, 256, 512), BF16)],
    )


def trail_kernel(rows, first, scale, tiles, early_both, late_both, *refs):
    t_buf, sems = refs[-2:]
    outs = refs[-2 - len(rows[2]) : -2]
    count = t_buf.shape[0]
    copies = fetch([(tiles.at[first[i], :, pl.ds(rows[0], rows[1])], t_buf.at[i]) for i in range(count)], sems)
    i = 0
    for n, out in zip(rows[2], outs):
        for block in range(n):
            copies[i].wait()
            total = None
            for k in range(STEPS):
                own = t_buf[i, k]
                value = early_both[k] if k < 5 else late_both[0]
                part = dot(jnp.concatenate([own, own], axis=1), value) * scale[first[i], k]
                total = part if total is None else total + part
            out[block] = total
            i += 1


def trail(first, scale, tiles, early_both, late_both, rows, mib, *after):
    count = sum(rows[2])
    return call(
        functools.partial(trail_kernel, rows),
        "trail",
        mib,
        [(S, first), (S, scale), (H, tiles), (V, early_both), (V, late_both)] + [(H, a) for a in after],
        [((n, rows[1], 512), F32) for n in rows[2]],
        [pltpu.VMEM((count, 6, rows[1], 128), BF16), pltpu.SemaphoreType.DMA((count,))],
        max(1, count * rows[1] // 256),
    )


def sum_sub_kernel(where, *refs):
    for h in range(2):
        a, b, c = refs[3 * h : 3 * h + 3]
        outs = refs[6 + 5 * h : 11 + 5 * h]

        def rows(e):
            at = lax.rem(where[h] + e, 4)
            return a[at] + (b[at] + c[at])

        outs[0][...] = rows(0)
        outs[1][...] = rows(1)
        outs[2][...] = rows(3)
        far = rows(2)
        outs[3][...] = far[: RING // 4]
        outs[4][...] = far[RING // 4 :]


def sum_sub(where, parts):
    outputs = [((RING // 2, 512), F32)] * 3 + [((RING // 4, 512), F32)] * 2
    return call(sum_sub_kernel, "sum_sub", 32, [(S, where)] + [(V, p) for p in parts], outputs * 2)


def finish_kernel(at, rhs, *refs):
    parts, outs, buf, sems = refs[:6], refs[6:8], refs[8], refs[9]
    copies = fetch(
        [(rhs.at[at[2 * h], pl.ds(pl.multiple_of(at[2 * h + 1] * (RING // 2), 8), RING // 2)], buf.at[h]) for h in range(2)], sems
    )
    for h in range(2):
        a, b, c = parts[3 * h : 3 * h + 3]
        copies[h].wait()
        outs[h][...] = buf[h] - (a[...] + (b[...] + c[...]))


def finish(at, rhs, parts):
    return call(
        finish_kernel,
        "finish",
        54,
        [(S, at), (H, rhs)] + [(V, p) for p in parts],
        [((RING // 2, 512), F32)] * 2,
        [pltpu.VMEM((2, RING // 2, 512), F32), pltpu.SemaphoreType.DMA((2,))],
    )


def place_kernel(where, *refs):
    for h in range(2):
        own, back, ahead, low, high = refs[5 * h : 5 * h + 5]
        out = refs[10 + h]
        for e, ref in ((0, own), (3, back), (1, ahead)):
            out[lax.rem(where[h] + e, 4)] = ref[...]
        far = lax.rem(where[h] + 2, 4)
        out[far, pl.ds(0, RING // 4), :] = low[...]
        out[far, pl.ds(RING // 4, RING // 4), :] = high[...]


def place(where, parts):
    return call(place_kernel, "place", 16, [(S, where)] + [(V, p) for p in parts], [((4, RING // 2, 512), F32)] * 2)


def on_device(rhs_blocks, factor_tiles, tile_scale, diag_inverse):
    row, column = lax.axis_index("prow"), lax.axis_index("pcol")
    y, u, z, x = row // 2, row % 2, column // 4, column % 4
    meta = jnp.stack([x, y, u, z]).astype(jnp.int32)
    tiles = jnp.transpose(factor_tiles, (0, 2, 1, 3))

    def shift(value, axis, d):
        if axis == "x":
            return lax.ppermute(value, "pcol", [(i, i // 4 * 4 + (i + d) % 4) for i in range(16)])
        if axis == "z":
            return lax.ppermute(value, "pcol", [(i, (i + 4 * d) % 16) for i in range(16)])
        if axis == "y":
            return lax.ppermute(value, "prow", [(i, (i + 2 * d) % 8) for i in range(8)])
        return lax.ppermute(value, "prow", [(i, i ^ 1) for i in range(8)])

    def exchange(values, axis):
        return [values[0]] + [shift(values[d], axis, d) for d in (1, 2, 3)]

    def spread(value, axis):
        return exchange([value] * 4, axis)

    def ring(values):
        return [(shift(up, axis, 1), shift(down, axis, 3)) for axis, up, down in values]

    def ring_z(value):
        half = value.shape[0] // 2
        near = ring([("z", value, value)])[0]
        far = ring([("z", near[0][:half], near[1][half:])])[0]
        return (value,) + near + far

    def make(rows, extra, whole, *after):
        return gram(rows, extra, whole, meta, tile_scale, diag_inverse, rhs_blocks, tiles, *after)

    def gather(piece):
        both = jnp.stack([piece, shift(piece, "core", 1)])
        return spread(both, "y")

    keep, send = make((1, 2), (0,), False)
    half = keep + shift(send, "core", 1)
    a, b, c, d = exchange([half[i] for i in range(4)], "y")
    total = (a + b) + (c + d)
    start = {0: total[:4], 1: total[4:8], 2: total[8:12]}
    a, b, c, d = spread(total[12:28], "z")
    grams = {1: (a, b, d, c), 2: ring_z(total[28:])}

    total = lax.psum_scatter(make((3, 4), (), True, half)[0], "prow")
    start[3], start[4] = total[:4], total[4:8]
    grams[3], grams[4] = ring_z(total[8:56]), ring_z(total[56:])

    solved = []
    piece = start[0]
    for s in range(1, STEPS):
        pieces = gather(piece)
        chunks, latest = step(meta, pieces, solved, grams[s])
        if s == 1:
            total = lax.psum_scatter(make((5,), (), True, chunks[0])[0], "prow")
            start[5] = total[:4]
            grams[5] = ring_z(total[4:])
        solved.append(latest)
        a, b, c, d = exchange(chunks, "x")
        piece = start[s] - ((a + b) + (c + d))

    others = exchange([jnp.stack([v[-d % 4] for v in solved]) for d in range(4)], "z")[1:]
    solved_early, both_early = early(meta, solved, others)
    piece = jnp.stack(exchange([piece[-d % 4] for d in range(4)], "z"))
    solved_late, both_late = late(meta, gather(piece), both_early)

    axes = (("x", "z", x, z, 6), ("z", "x", z, x, 14))
    one, two = [a[0] for a in axes], [a[1] for a in axes]
    where = jnp.stack([a[3] for a in axes]).astype(jnp.int32)

    operands = (tile_scale, tiles, both_early, both_late)
    shared = trail(jnp.arange(6, 22, dtype=jnp.int32), *operands, (RING, 256 - RING, (16,)), 56)[0]
    summed = lax.psum(shared, "pcol")

    def chunks_of(offsets, blocks, mib, after):
        first = jnp.stack([base + 2 * ((me + d) % 4) + i for d in offsets for _, _, me, _, base in axes for i in range(2)])
        rows = (0, RING, (blocks,) * (4 * len(offsets) // blocks))
        return trail(first.astype(jnp.int32), *operands, rows, mib, after)

    far = chunks_of((2,), 1, 56, shared)
    near = chunks_of((1, 3, 0), 2, 24, far[0])
    moved = ring([(one[h], far[2 * h], far[2 * h + 1]) for h in range(2)])
    ups = [near[h].at[:1].add(moved[h][0]) for h in range(2)]
    downs = [near[2 + h].at[1:].add(moved[h][1]) for h in range(2)]
    moved = ring([(one[h], ups[h], downs[h]) for h in range(2)])
    terms = [v.reshape(4, RING // 2, 512) for h in range(2) for v in (near[4 + h],) + moved[h]]
    subs = sum_sub(where, terms)
    subs = [subs[:5], subs[5:]]
    moved = ring([(two[h], subs[h][3], subs[h][4]) for h in range(2)])
    ups = [subs[h][1].at[: RING // 4].add(moved[h][0]) for h in range(2)]
    downs = [subs[h][2].at[RING // 4 :].add(moved[h][1]) for h in range(2)]
    moved = ring([(two[h], ups[h], downs[h]) for h in range(2)])
    at = jnp.stack([v for _, _, me, other, base in axes for v in (base + 2 * me + other // 2, other % 2)])
    done = finish(at.astype(jnp.int32), rhs_blocks, [v for h in range(2) for v in (subs[h][0],) + moved[h]])
    near = ring([(two[h], done[h], done[h]) for h in range(2)])
    far = ring([(two[h], near[h][0][: RING // 4], near[h][1][RING // 4 :]) for h in range(2)])
    own = place(where, [v for h in range(2) for v in (done[h],) + near[h] + far[h]])
    own = [v.reshape(2, RING, 512) for v in own]
    near = ring([(one[h], own[h], own[h]) for h in range(2)])
    far = ring([(one[h], near[h][0][:1], near[h][1][1:]) for h in range(2)])
    trailing = jnp.zeros((16, 256, 512), F32)
    for h, (_, _, me, _, base) in enumerate(axes):
        for d, value in ((0, own[h]), (3, near[h][0]), (1, near[h][1])):
            trailing = lax.dynamic_update_slice(trailing, value, (base - 6 + 2 * ((me + d) % 4), 0, 0))
    trailing = lax.dynamic_update_slice(trailing, rhs_blocks[6:, RING:] - summed, (0, RING, 0))
    for h, (_, _, me, _, base) in enumerate(axes):
        for i in range(2):
            trailing = lax.dynamic_update_slice(trailing, far[h][i], (base - 6 + 2 * ((me + 2) % 4) + i, 0, 0))
    return jnp.concatenate([solved_early, solved_late]), trailing


def solution(mesh):
    in_specs = (P(None, "prow", None), P(None, "prow", None, "pcol"), P(), P(None, None, "prow"))
    out_specs = (P(None, "pcol", None), P(None, "prow", None))
    return jax.shard_map(
        on_device, mesh=mesh, in_specs=in_specs, out_specs=out_specs, check_vma=False
    )
```

```python
import functools

import jax
import jax.numpy as jnp
from jax import lax
from jax.experimental import pallas as pl
from jax.experimental.pallas import tpu as pltpu
from jax.sharding import PartitionSpec as P

F32 = jnp.float32
BF16 = jnp.bfloat16
STEPS = 6
RING = 160
V, H, S = (pl.BlockSpec(memory_space=m) for m in (pltpu.VMEM, pltpu.HBM, pltpu.SMEM))


def split(value):
    high = value.astype(BF16)
    return high, (value - high.astype(F32)).astype(BF16)


def dot(a, b):
    return jnp.dot(a, b, preferred_element_type=F32)


def call(kernel, name, mib, inputs, outputs, scratch=(), blocks=0):
    specs, operands = zip(*inputs)
    return pl.pallas_call(
        kernel,
        in_specs=specs,
        out_specs=[V] * len(outputs),
        out_shape=[jax.ShapeDtypeStruct(*o) for o in outputs],
        scratch_shapes=scratch,
        compiler_params=pltpu.CompilerParams(vmem_limit_bytes=mib << 20),
        cost_estimate=pl.CostEstimate(flops=0, bytes_accessed=blocks << 22, transcendentals=0) if blocks else None,
        name=name,
    )(*operands)


def fetch(pairs, sems):
    copies = [pltpu.make_async_copy(a, b, sems.at[i]) for i, (a, b) in enumerate(pairs)]
    for copy in copies:
        copy.start()
    return copies


def gram_kernel(rows, extra, whole, meta, scale, inverse, rhs, tiles, *refs):
    outs = refs[-6:-5] if whole else refs[-7:-5]
    d_buf, r_buf, t_buf, product, sems = refs[-5:]
    x, y, u, z = meta[0], meta[1], meta[2], meta[3]
    blocks = extra + rows
    group = pl.ds(pl.multiple_of(z * 128, 128), 128)
    copies = []
    sem = 0
    for i, b in enumerate(blocks):
        copies.append(fetch([(inverse.at[b], d_buf.at[i]), (rhs.at[b, :, group], r_buf.at[i])], sems.at[pl.ds(sem, 2)]))
        sem += 2
    base = 0
    for s in rows:
        copies[len(extra) + rows.index(s)] += fetch(
            [(tiles.at[s, pl.ds(0, s)], t_buf.at[pl.ds(base, s)])], sems.at[pl.ds(sem, 1)]
        )
        sem += 1
        base += s

    def store(slot, row, at):
        for yy in range(4):
            if whole:
                for core in range(2):
                    outs[0][2 * yy + core, at] = product[slot, pl.ds(pl.multiple_of(row + yy * 32 + core * 16, 16), 16), :]
            else:
                ey = lax.rem(yy + 4 - y, 4) if extra else yy
                start = row + yy * 32
                outs[0][ey, at] = product[slot, pl.ds(pl.multiple_of(start + u * 16, 16), 16), :]
                outs[1][ey, at] = product[slot, pl.ds(pl.multiple_of(start + (1 - u) * 16, 16), 16), :]

    turn = 0
    base = 0
    unit = 4 * len(blocks)
    for i, b in enumerate(blocks):
        for copy in copies[i]:
            copy.wait()
        high, low = split(r_buf[i])
        both = jnp.concatenate([high, low], axis=0)
        slot = turn % 2
        turn += 1
        for dz in range(4):
            chunk = lax.rem(z + 4 - dz, 4) * 4 + x
            part = d_buf[i, pl.ds(pl.multiple_of(chunk * 128, 128), 128), :]
            product[slot, pl.ds(dz * 128, 128), :] = dot(jnp.concatenate([part, part], axis=1), both)
            store(slot, dz * 128, i * 4 + dz)
        if b not in rows:
            continue
        for j in range(b):
            slot = turn % 2
            turn += 1
            product[slot] = dot(d_buf[i], t_buf[base]) * scale[j, b]
            base += 1
            for zz in range(4):
                for ex in range(4):
                    store(slot, (zz * 4 + lax.rem(x + ex, 4)) * 128, unit + ex * 4 + zz)
            unit += 16


def gram(rows, extra, whole, meta, scale, inverse, rhs, tiles, *after):
    n = len(extra) + len(rows)
    units = 4 * n + 16 * sum(rows)
    outputs = [((8, units, 16, 128), F32)] if whole else [((4, units, 16, 128), F32)] * 2
    return call(
        functools.partial(gram_kernel, rows, extra, whole),
        "gram",
        58,
        [(S, meta), (S, scale), (H, inverse), (H, rhs), (H, tiles)] + [(H, a) for a in after],
        outputs,
        [
            pltpu.VMEM((n, 2048, 256), BF16),
            pltpu.VMEM((n, 256, 128), F32),
            pltpu.VMEM((sum(rows), 256, 128), BF16),
            pltpu.VMEM((2, 2048, 128), F32),
            pltpu.SemaphoreType.DMA((2 * n + len(rows),)),
        ],
        sum(rows) + 2,
    )


def step_kernel(count, unused, meta, *refs):
    y, u, z = meta[1], meta[2], meta[3]
    pieces, refs = refs[:4], refs[4:]
    older, refs = refs[: count - 1], refs[count - 1 :]
    gram_refs, refs = refs[: len(refs) - 7 - unused], refs[-7:]
    chunks, solved, g_buf, sems = refs[:4], refs[4], refs[5], refs[6]
    targets = [g_buf.at[d] for d in (0, 1, 3, 2)]
    if len(gram_refs) == 5:
        targets[3:] = [g_buf.at[2, pl.ds(0, 8 * count)], g_buf.at[2, pl.ds(8 * count, 8 * count)]]
    copies = fetch(list(zip(gram_refs, targets)), sems)
    for ey in range(4):
        row = lax.rem(y + 4 - ey, 4) * 32
        for eu in range(2):
            at = pl.multiple_of(row + (u + eu - 2 * u * eu) * 16, 16)
            for dz in range(4):
                solved[dz, pl.ds(at, 16), :] = pieces[ey][eu, dz]
    for copy in copies:
        copy.wait()
    total = jnp.zeros((256, 128), F32)
    for j in range(count):
        block = jnp.concatenate([g_buf[d, pl.ds(16 * j, 16)].reshape(256, 128) for d in range(4)], axis=1)
        source = solved if j == count - 1 else older[j]
        a_high, a_low = split(block)
        b_high, b_low = split(source[...].reshape(512, 128))
        total = total + (dot(a_high, b_high) + (dot(a_high, b_low) + dot(a_low, b_high)))
    total = total.reshape(4, 4, 16, 128)
    for ex in range(4):
        for zz in range(4):
            chunks[ex][lax.rem(z + 4 - zz, 4)] = total[ex, zz]


def step(meta, pieces, older, pieces_z, after):
    count = len(older) + 1
    *chunks, solved = call(
        functools.partial(step_kernel, count, len(after)),
        "step",
        24,
        [(S, meta)] + [(V, p) for p in pieces] + [(V, o) for o in older] + [(H, g) for g in pieces_z] + [(H, a) for a in after],
        [((4, 16, 128), F32)] * 4 + [((4, 128, 128), F32)],
        [pltpu.VMEM((4, 16 * count, 16, 128), F32), pltpu.SemaphoreType.DMA((5,))],
    )
    return chunks, solved


def early_kernel(meta, *refs):
    z = meta[3]
    own, others, solved, both = refs[:4], refs[4:7], refs[7], refs[8]
    for k in range(4):
        for d in range(4):
            group = pl.ds(pl.multiple_of(lax.rem(z + 4 - d, 4) * 128, 128), 128)
            value = own[k][0] if d == 0 else others[d - 1][k]
            high, low = split(value)
            solved[k, :, group] = value
            both[k, pl.ds(0, 128), group] = high
            both[k, pl.ds(128, 128), group] = low


def early(meta, own, others):
    return call(
        early_kernel,
        "early",
        16,
        [(S, meta)] + [(V, o) for o in own] + [(V, o) for o in others],
        [((4, 128, 512), F32), ((4, 256, 512), BF16)],
    )


def late_kernel(meta, a, b, c, d, w0, w1, w2, w3, solved, both):
    y, u, z = meta[1], meta[2], meta[3]
    for dz, ref in enumerate((w0, w1, w2, w3)):
        group = pl.ds(pl.multiple_of(lax.rem(z + 4 - dz, 4) * 128, 128), 128)
        value = ref[pl.ds(16, 128), :]
        high, low = split(value)
        solved[0, :, group] = value
        both[0, pl.ds(0, 128), group] = high
        both[0, pl.ds(128, 128), group] = low
    for ey, piece in enumerate((a, b, c, d)):
        row = lax.rem(y + 4 - ey, 4) * 32
        for eu in range(2):
            at = pl.multiple_of(row + (u + eu - 2 * u * eu) * 16, 16)
            low_at = pl.multiple_of(at + 128, 16)
            for dz in range(4):
                group = pl.ds(pl.multiple_of(lax.rem(z + 4 - dz, 4) * 128, 128), 128)
                value = piece[eu, dz]
                high, low = split(value)
                solved[1, pl.ds(at, 16), group] = value
                both[1, pl.ds(at, 16), group] = high
                both[1, pl.ds(low_at, 16), group] = low


def late(meta, pieces, groups):
    return call(
        late_kernel,
        "late",
        8,
        [(S, meta)] + [(V, p) for p in pieces] + [(V, g) for g in groups],
        [((2, 128, 512), F32), ((2, 256, 512), BF16)],
    )


def trail_kernel(rows, first, scale, tiles, early_both, late_both, *refs):
    t_buf, sems = refs[-2:]
    outs = refs[-2 - len(rows[2]) : -2]
    count = t_buf.shape[0]
    copies = fetch([(tiles.at[first[i], :, pl.ds(rows[0], rows[1])], t_buf.at[i]) for i in range(count)], sems)
    places = [(out, block) for n, out in zip(rows[2], outs) for block in range(n)]
    stack = 4 if rows[1] > 128 else 16
    for base in range(0, count, stack):
        for i in range(base, base + stack):
            copies[i].wait()
        for k in range(STEPS):
            own = t_buf[pl.ds(base, stack), k].reshape(stack * rows[1], 128)
            value = early_both[k] if k < 4 else late_both[k - 4]
            part = dot(jnp.concatenate([own, own], axis=1), value)
            for i in range(stack):
                out, block = places[base + i]
                term = part[i * rows[1] : (i + 1) * rows[1]] * scale[k, first[base + i]]
                out[block] = term if k == 0 else out[block] + term


def trail(first, scale, tiles, early_both, late_both, rows, mib, *after):
    count = sum(rows[2])
    return call(
        functools.partial(trail_kernel, rows),
        "trail",
        mib,
        [(S, first), (S, scale), (H, tiles), (V, early_both), (V, late_both)] + [(H, a) for a in after],
        [((n, rows[1], 512), F32) for n in rows[2]],
        [pltpu.VMEM((count, 6, rows[1], 128), BF16), pltpu.SemaphoreType.DMA((count,))],
        max(1, count * rows[1] // 256),
    )


def sum_sub_kernel(where, *refs):
    for h in range(2):
        a, b, c = refs[3 * h : 3 * h + 3]
        outs = refs[6 + 5 * h : 11 + 5 * h]

        def rows(e):
            at = lax.rem(where[h] + e, 4)
            return a[at] + (b[at] + c[at])

        outs[0][...] = rows(0)
        outs[1][...] = rows(1)
        outs[2][...] = rows(3)
        far = rows(2)
        outs[3][...] = far[: RING // 4]
        outs[4][...] = far[RING // 4 :]


def sum_sub(where, parts):
    outputs = [((RING // 2, 512), F32)] * 3 + [((RING // 4, 512), F32)] * 2
    return call(sum_sub_kernel, "sum_sub", 32, [(S, where)] + [(V, p) for p in parts], outputs * 2)


def place_kernel(where, *refs):
    for h in range(2):
        own, back, ahead, low, high = refs[5 * h : 5 * h + 5]
        out = refs[10 + h]
        for e, ref in ((0, own), (3, back), (1, ahead)):
            out[lax.rem(where[h] + e, 4)] = ref[...]
        far = lax.rem(where[h] + 2, 4)
        out[far, pl.ds(0, RING // 4), :] = low[...]
        out[far, pl.ds(RING // 4, RING // 4), :] = high[...]


def place(where, parts):
    return call(place_kernel, "place", 16, [(S, where)] + [(V, p) for p in parts], [((4, RING // 2, 512), F32)] * 2)


def on_device(rhs_blocks, factor_tiles, tile_scale, diag_inverse):
    row, column = lax.axis_index("prow"), lax.axis_index("pcol")
    y, u, z, x = row // 2, row % 2, column // 4, column % 4
    meta = jnp.stack([x, y, u, z]).astype(jnp.int32)
    tiles = jnp.transpose(factor_tiles, (0, 2, 1, 3))
    scale = jnp.transpose(tile_scale)

    def shift(value, axis, d):
        if axis == "x":
            return lax.ppermute(value, "pcol", [(i, i // 4 * 4 + (i + d) % 4) for i in range(16)])
        if axis == "z":
            return lax.ppermute(value, "pcol", [(i, (i + 4 * d) % 16) for i in range(16)])
        if axis == "y":
            return lax.ppermute(value, "prow", [(i, (i + 2 * d) % 8) for i in range(8)])
        return lax.ppermute(value, "prow", [(i, i ^ 1) for i in range(8)])

    def exchange(values, axis):
        return [values[0]] + [shift(values[d], axis, d) for d in (1, 2, 3)]

    def spread(value, axis):
        return exchange([value] * 4, axis)

    def ring(values):
        return [(shift(up, axis, 1), shift(down, axis, 3)) for axis, up, down in values]

    def ring_z(value):
        half = value.shape[0] // 2
        near = ring([("z", value, value)])[0]
        far = ring([("z", near[0][:half], near[1][half:])])[0]
        return (value,) + near + far

    def make(rows, extra, whole, *after):
        return gram(rows, extra, whole, meta, scale, diag_inverse, rhs_blocks, tiles, *after)

    def gather(piece):
        both = jnp.stack([piece, shift(piece, "core", 1)])
        return spread(both, "y")

    keep, send = make((1, 2), (0,), False)
    half = keep + shift(send, "core", 1)
    a, b, c, d = exchange([half[i] for i in range(4)], "y")
    total = (a + b) + (c + d)
    start = {0: total[:4], 1: total[4:8], 2: total[8:12]}
    a, b, c, d = spread(total[12:28], "z")
    grams = {1: (a, b, d, c), 2: ring_z(total[28:])}

    total = lax.psum_scatter(make((3, 4), (), True, keep)[0], "prow")
    start[3], start[4] = total[:4], total[4:8]
    grams[3], grams[4] = ring_z(total[8:56]), ring_z(total[56:])

    solved = []
    piece = start[0]
    for s in range(1, STEPS):
        pieces = gather(piece)
        if s == 2:
            total = lax.psum_scatter(make((5,), (), True, pieces[0])[0], "prow")
            start[5] = total[:4]
            grams[5] = ring_z(total[4:])
        if s == 5:
            others = exchange([jnp.stack([v[-d % 4] for v in solved]) for d in range(4)], "z")[1:]
            solved_early, both_early = early(meta, solved, others)
        after = grams[2][1:] if s == 1 else grams[s + 1][1:3] if s < 5 else (both_early,)
        chunks, latest = step(meta, pieces, solved, grams[s], after)
        solved.append(latest)
        a, b, c, d = exchange(chunks, "x")
        piece = start[s] - ((a + b) + (c + d))

    groups = exchange([jnp.concatenate([piece[-d % 4], latest[-d % 4]]) for d in range(4)], "z")
    solved_late, both_late = late(meta, gather(jnp.stack([g[:16] for g in groups])), groups)

    axes = (("x", "z", x, z, 6), ("z", "x", z, x, 14))
    one, two = [a[0] for a in axes], [a[1] for a in axes]
    where = jnp.stack([a[3] for a in axes]).astype(jnp.int32)

    operands = (scale, tiles, both_early, both_late)
    shared = trail(jnp.arange(6, 22, dtype=jnp.int32), *operands, (RING, 256 - RING, (16,)), 56)[0]
    summed = lax.psum(shared, "pcol")

    def chunks_of(offsets, blocks, mib, after):
        first = jnp.stack([base + 2 * ((me + d) % 4) + i for d in offsets for _, _, me, _, base in axes for i in range(2)])
        rows = (0, RING, (blocks,) * (4 * len(offsets) // blocks))
        return trail(first.astype(jnp.int32), *operands, rows, mib, after)

    far = chunks_of((2,), 1, 56, shared)
    near = chunks_of((1, 3, 0), 2, 24, far[0])
    moved = ring([(one[h], far[2 * h], far[2 * h + 1]) for h in range(2)])
    ups = [near[h].at[:1].add(moved[h][0]) for h in range(2)]
    downs = [near[2 + h].at[1:].add(moved[h][1]) for h in range(2)]
    moved = ring([(one[h], ups[h], downs[h]) for h in range(2)])
    terms = [v.reshape(4, RING // 2, 512) for h in range(2) for v in (near[4 + h],) + moved[h]]
    subs = sum_sub(where, terms)
    subs = [subs[:5], subs[5:]]
    moved = ring([(two[h], subs[h][3], subs[h][4]) for h in range(2)])
    ups = [subs[h][1].at[: RING // 4].add(moved[h][0]) for h in range(2)]
    downs = [subs[h][2].at[RING // 4 :].add(moved[h][1]) for h in range(2)]
    moved = ring([(two[h], ups[h], downs[h]) for h in range(2)])
    done = []
    for h, (_, _, me, other, base) in enumerate(axes):
        at = (base + 2 * me + other // 2, other % 2 * (RING // 2), 0)
        mine = lax.dynamic_slice(rhs_blocks, at, (1, RING // 2, 512))[0]
        done.append(mine - (subs[h][0] + (moved[h][0] + moved[h][1])))
    near = ring([(two[h], done[h], done[h]) for h in range(2)])
    far = ring([(two[h], near[h][0][: RING // 4], near[h][1][RING // 4 :]) for h in range(2)])
    own = place(where, [v for h in range(2) for v in (done[h],) + near[h] + far[h]])
    own = [v.reshape(2, RING, 512) for v in own]
    near = ring([(one[h], own[h], own[h]) for h in range(2)])
    far = ring([(one[h], near[h][0][:1], near[h][1][1:]) for h in range(2)])
    trailing = jnp.zeros((16, 256, 512), F32)
    for h, (_, _, me, _, base) in enumerate(axes):
        for d, value in ((0, own[h]), (3, near[h][0]), (1, near[h][1])):
            trailing = lax.dynamic_update_slice(trailing, value, (base - 6 + 2 * ((me + d) % 4), 0, 0))
    trailing = lax.dynamic_update_slice(trailing, rhs_blocks[6:, RING:] - summed, (0, RING, 0))
    for h, (_, _, me, _, base) in enumerate(axes):
        for i in range(2):
            trailing = lax.dynamic_update_slice(trailing, far[h][i], (base - 6 + 2 * ((me + 2) % 4) + i, 0, 0))
    return jnp.concatenate([solved_early, solved_late]), trailing


def solution(mesh):
    in_specs = (P(None, "prow", None), P(None, "prow", None, "pcol"), P(), P(None, None, "prow"))
    out_specs = (P(None, "pcol", None), P(None, "prow", None))
    return jax.shard_map(
        on_device, mesh=mesh, in_specs=in_specs, out_specs=out_specs, check_vma=False
    )
```

```python
import functools

import jax
import jax.numpy as jnp
from jax import lax
from jax.experimental import pallas as pl
from jax.experimental.pallas import tpu as pltpu
from jax.sharding import PartitionSpec as P

F32 = jnp.float32
BF16 = jnp.bfloat16
STEPS = 6
RING = 128
V, H, S = (pl.BlockSpec(memory_space=m) for m in (pltpu.VMEM, pltpu.HBM, pltpu.SMEM))


def split(value):
    high = value.astype(BF16)
    return high, (value - high.astype(F32)).astype(BF16)


def dot(a, b):
    return jnp.dot(a, b, preferred_element_type=F32)


def call(kernel, name, mib, inputs, outputs, scratch=(), blocks=0):
    specs, operands = zip(*inputs)
    return pl.pallas_call(
        kernel,
        in_specs=specs,
        out_specs=[V] * len(outputs),
        out_shape=[jax.ShapeDtypeStruct(*o) for o in outputs],
        scratch_shapes=scratch,
        compiler_params=pltpu.CompilerParams(vmem_limit_bytes=mib << 20),
        cost_estimate=pl.CostEstimate(flops=0, bytes_accessed=blocks << 22, transcendentals=0) if blocks else None,
        name=name,
    )(*operands)


def fetch(pairs, sems):
    copies = [pltpu.make_async_copy(a, b, sems.at[i]) for i, (a, b) in enumerate(pairs)]
    for copy in copies:
        copy.start()
    return copies


def gram_kernel(rows, extra, whole, meta, scale, inverse, rhs, tiles, *refs):
    outs = refs[-6:-5] if whole else refs[-7:-5]
    d_buf, r_buf, t_buf, product, sems = refs[-5:]
    c, y, u = meta[0], meta[1], meta[2]
    blocks = extra + rows
    copies = []
    sem = 0
    for i, b in enumerate(blocks):
        copies.append(fetch([(inverse.at[b], d_buf.at[i]), (rhs.at[b], r_buf.at[i])], sems.at[pl.ds(sem, 2)]))
        sem += 2
    base = 0
    for s in rows:
        copies[len(extra) + rows.index(s)] += fetch(
            [(tiles.at[s, pl.ds(0, s)], t_buf.at[pl.ds(base, s)])], sems.at[pl.ds(sem, 1)]
        )
        sem += 1
        base += s

    def store(slot, row, at):
        for yy in range(4):
            if whole:
                for core in range(2):
                    outs[0][2 * yy + core, at] = product[slot, pl.ds(row + yy * 32 + core * 16, 16), :]
            else:
                ey = lax.rem(yy + 4 - y, 4)
                start = row + yy * 32
                outs[0][ey, at] = product[slot, pl.ds(pl.multiple_of(start + u * 16, 16), 16), :]
                outs[1][ey, at] = product[slot, pl.ds(pl.multiple_of(start + (1 - u) * 16, 16), 16), :]

    turn = 0
    base = 0
    unit = 4 * len(blocks)
    for i, b in enumerate(blocks):
        for copy in copies[i]:
            copy.wait()
        high, low = split(r_buf[i])
        both = jnp.concatenate([high, low], axis=0)
        part = d_buf[i, pl.ds(pl.multiple_of(c * 128, 128), 128), :]
        value = dot(jnp.concatenate([part, part], axis=1), both)
        slot = turn % 2
        turn += 1
        for g in range(4):
            product[slot, pl.ds(g * 128, 128), :] = value[:, g * 128 : (g + 1) * 128]
            store(slot, g * 128, i * 4 + g)
        if b not in rows:
            continue
        for j in range(b):
            slot = turn % 2
            turn += 1
            product[slot] = dot(d_buf[i], t_buf[base]) * scale[j, b]
            base += 1
            for chunk in range(16):
                store(slot, chunk * 128, unit + chunk)
            unit += 16


def gram(rows, extra, whole, meta, scale, inverse, rhs, tiles, *after):
    n = len(extra) + len(rows)
    units = 4 * n + 16 * sum(rows)
    outputs = [((8, units, 16, 128), F32)] if whole else [((4, units, 16, 128), F32)] * 2
    return call(
        functools.partial(gram_kernel, rows, extra, whole),
        "gram",
        58,
        [(S, meta), (S, scale), (H, inverse), (H, rhs), (H, tiles)] + [(H, a) for a in after],
        outputs,
        [
            pltpu.VMEM((n, 2048, 256), BF16),
            pltpu.VMEM((n, 256, 512), F32),
            pltpu.VMEM((sum(rows), 256, 128), BF16),
            pltpu.VMEM((2, 2048, 128), F32),
            pltpu.SemaphoreType.DMA((2 * n + len(rows),)),
        ],
        sum(rows) + 2,
    )


def join(meta, pieces, solved, both):
    y, u = meta[1], meta[2]
    for ey in range(4):
        row = lax.rem(y + 4 - ey, 4) * 32
        for eu in range(2):
            at = pl.multiple_of(row + (u + eu - 2 * u * eu) * 16, 16)
            value = pieces[ey][eu]
            high, low = split(value)
            solved[pl.ds(at, 16), :] = value
            both[pl.ds(at, 16), :] = high
            both[pl.ds(pl.multiple_of(at + 128, 16), 16), :] = low


def step_kernel(count, meta, *refs):
    pieces, older, blocks = refs[:4], refs[4 : 3 + count], refs[3 + count]
    terms, solved, both, g_buf, sem = refs[-5:]
    copy = pltpu.make_async_copy(blocks, g_buf, sem)
    copy.start()
    join(meta, pieces, solved, both)
    copy.wait()
    total = None
    for j in range(count):
        high, low = split(g_buf[pl.ds(16 * j, 16)].reshape(256, 128))
        source = both if j == count - 1 else older[j]
        part = dot(jnp.concatenate([high, high], axis=1), source[...]) + dot(low, source[pl.ds(0, 128), :])
        total = part if total is None else total + part
    terms[...] = total.reshape(16, 16, 512)


def step(meta, pieces, older, blocks, after):
    count = len(older) + 1
    return call(
        functools.partial(step_kernel, count),
        "step",
        24,
        [(S, meta)] + [(V, p) for p in pieces] + [(V, o) for o in older] + [(H, blocks)] + [(H, a) for a in after],
        [((16, 16, 512), F32), ((128, 512), F32), ((256, 512), BF16)],
        [pltpu.VMEM((16 * count, 16, 128), F32), pltpu.SemaphoreType.DMA],
    )


def last_kernel(meta, a, b, c, d, solved, both):
    join(meta, (a, b, c, d), solved, both)


def last(meta, pieces):
    inputs = [(S, meta)] + [(V, p) for p in pieces]
    return call(last_kernel, "last", 8, inputs, [((128, 512), F32), ((256, 512), BF16)])


def trail_kernel(groups, first, scale, tiles, *refs):
    both = refs[:STEPS]
    sems = refs[-1]
    buffers = refs[-1 - len(groups) : -1]
    outs = refs[-1 - len(groups) - sum(len(g[2]) for g in groups) : -1 - len(groups)]
    plan, copies, at = [], [], 0
    for (start, rows, sizes), buffer in zip(groups, buffers):
        count = sum(sizes)
        copies.append(
            fetch(
                [(tiles.at[first[at + i], :, pl.ds(start, rows)], buffer.at[i]) for i in range(count)],
                sems.at[pl.ds(at, count)],
            )
        )
        places = [(out, block) for n, out in zip(sizes, outs) for block in range(n)]
        outs = outs[len(sizes) :]
        plan.append((rows, buffer, places, at))
        at += count
    for (rows, buffer, places, at), waits in zip(plan, copies):
        stack = min(len(places), 8)
        for base in range(0, len(places), stack):
            size = min(stack, len(places) - base)
            for i in range(size):
                waits[base + i].wait()
            for k in range(STEPS):
                own = buffer[pl.ds(base, size), k].reshape(size * rows, 128)
                part = dot(jnp.concatenate([own, own], axis=1), both[k][...])
                for i in range(size):
                    out, block = places[base + i]
                    term = part[i * rows : (i + 1) * rows] * scale[k, first[at + base + i]]
                    out[block] = term if k == 0 else out[block] + term


def trail(first, scale, tiles, both, groups, mib, *after):
    count = first.shape[0]
    return call(
        functools.partial(trail_kernel, groups),
        "trail",
        mib,
        [(S, first), (S, scale), (H, tiles)] + [(V, v) for v in both] + [(H, a) for a in after],
        [((n, rows, 512), F32) for _, rows, sizes in groups for n in sizes],
        [pltpu.VMEM((sum(sizes), 6, rows, 128), BF16) for _, rows, sizes in groups] + [pltpu.SemaphoreType.DMA((count,))],
        max(1, sum(rows * sum(sizes) for _, rows, sizes in groups) // 256),
    )


def sum_sub_kernel(where, *refs):
    for h in range(2):
        a, b, c = refs[3 * h : 3 * h + 3]
        outs = refs[6 + 5 * h : 11 + 5 * h]

        def rows(e):
            at = lax.rem(where[h] + e, 4)
            return a[at] + (b[at] + c[at])

        outs[0][...] = rows(0)
        outs[1][...] = rows(1)
        outs[2][...] = rows(3)
        far = rows(2)
        outs[3][...] = far[: RING // 4]
        outs[4][...] = far[RING // 4 :]


def sum_sub(where, parts):
    outputs = [((RING // 2, 512), F32)] * 3 + [((RING // 4, 512), F32)] * 2
    return call(sum_sub_kernel, "sum_sub", 32, [(S, where)] + [(V, p) for p in parts], outputs * 2)


def place_kernel(where, *refs):
    for h in range(2):
        own, back, ahead, low, high = refs[5 * h : 5 * h + 5]
        out = refs[11 + h]
        for e, ref in ((0, own), (3, back), (1, ahead)):
            out[lax.rem(where[h] + e, 4)] = ref[...]
        far = lax.rem(where[h] + 2, 4)
        out[far, pl.ds(0, RING // 4), :] = low[...]
        out[far, pl.ds(RING // 4, RING // 4), :] = high[...]


def place(where, parts, after):
    return call(place_kernel, "place", 16, [(S, where)] + [(V, p) for p in parts] + [(H, after)], [((4, RING // 2, 512), F32)] * 2)


def on_device(rhs_blocks, factor_tiles, tile_scale, diag_inverse):
    row, column = lax.axis_index("prow"), lax.axis_index("pcol")
    y, u, z, x = row // 2, row % 2, column // 4, column % 4
    meta = jnp.stack([column, y, u]).astype(jnp.int32)
    tiles = jnp.transpose(factor_tiles, (0, 2, 1, 3))
    scale = jnp.transpose(tile_scale)

    def shift(value, axis, d):
        if axis == "x":
            return lax.ppermute(value, "pcol", [(i, i // 4 * 4 + (i + d) % 4) for i in range(16)])
        if axis == "z":
            return lax.ppermute(value, "pcol", [(i, (i + 4 * d) % 16) for i in range(16)])
        if axis == "y":
            return lax.ppermute(value, "prow", [(i, (i + 2 * d) % 8) for i in range(8)])
        return lax.ppermute(value, "prow", [(i, i ^ 1) for i in range(8)])

    def exchange(values, axis):
        return [values[0]] + [shift(values[d], axis, d) for d in (1, 2, 3)]

    def spread(value, axis):
        return exchange([value] * 4, axis)

    def ring(values):
        return [(shift(up, axis, 1), shift(down, axis, 3)) for axis, up, down in values]

    def make(rows, extra, whole, *after):
        return gram(rows, extra, whole, meta, scale, diag_inverse, rhs_blocks, tiles, *after)

    def gather(piece):
        both = jnp.stack([piece, shift(piece, "core", 1)])
        return spread(both, "y")

    def ends(total, blocks):
        for i, b in enumerate(blocks):
            start[b] = jnp.transpose(total[4 * i : 4 * i + 4], (1, 0, 2)).reshape(16, 512)

    start, grams = {}, {}
    keep, send = make((1,), (0,), False)
    half = keep + shift(send, "core", 1)
    a, b, c, d = exchange([half[i] for i in range(4)], "y")
    total = (a + b) + (c + d)
    ends(total, (0, 1))
    grams[1] = total[8:]
    products = keep
    for rows in ((2, 3), (4, 5)):
        products = make(rows, (), True, products)[0]
        total = lax.psum_scatter(products, "prow")
        ends(total, rows)
        grams[rows[0]], grams[rows[1]] = total[8 : 8 + 16 * rows[0]], total[8 + 16 * rows[0] :]

    solved, both = [], []
    piece = start[0]
    for s in range(1, STEPS):
        terms, latest, parts = step(meta, gather(piece), both, grams[s], (products,) if s == 1 else ())
        solved.append(latest)
        both.append(parts)
        terms = lax.all_to_all(terms, "pcol", 0, 0)
        piece = start[s] - jnp.sum(terms, axis=0)
    latest, parts = last(meta, gather(piece))
    solved.append(latest)
    both.append(parts)

    axes = (("x", "z", x, z, 6), ("z", "x", z, x, 14))
    one, two = [a[0] for a in axes], [a[1] for a in axes]
    where = jnp.stack([a[3] for a in axes]).astype(jnp.int32)

    def chunks_of(offsets):
        return [base + 2 * ((me + d) % 4) + i for d in offsets for _, _, me, _, base in axes for i in range(2)]

    first = jnp.stack(list(range(6, 22)) + chunks_of((2,))).astype(jnp.int32)
    groups = ((RING, 256 - RING, (16,)), (0, RING, (1,) * 4))
    shared, *far = trail(first, scale, tiles, both, groups, 56)
    summed = lax.psum(shared, "pcol")
    first = jnp.stack(chunks_of((1, 3, 0))).astype(jnp.int32)
    near = trail(first, scale, tiles, both, ((0, RING, (2,) * 6),), 24, far[0])
    moved = ring([(one[h], far[2 * h], far[2 * h + 1]) for h in range(2)])
    ups = [near[h].at[:1].add(moved[h][0]) for h in range(2)]
    downs = [near[2 + h].at[1:].add(moved[h][1]) for h in range(2)]
    moved = ring([(one[h], ups[h], downs[h]) for h in range(2)])
    terms = [v.reshape(4, RING // 2, 512) for h in range(2) for v in (near[4 + h],) + moved[h]]
    subs = sum_sub(where, terms)
    subs = [subs[:5], subs[5:]]
    moved = ring([(two[h], subs[h][3], subs[h][4]) for h in range(2)])
    ups = [subs[h][1].at[: RING // 4].add(moved[h][0]) for h in range(2)]
    downs = [subs[h][2].at[RING // 4 :].add(moved[h][1]) for h in range(2)]
    moved = ring([(two[h], ups[h], downs[h]) for h in range(2)])
    done = []
    for h, (_, _, me, other, base) in enumerate(axes):
        at = (base + 2 * me + other // 2, other % 2 * (RING // 2), 0)
        mine = lax.dynamic_slice(rhs_blocks, at, (1, RING // 2, 512))[0]
        done.append(mine - (subs[h][0] + (moved[h][0] + moved[h][1])))
    near = ring([(two[h], done[h], done[h]) for h in range(2)])
    far = ring([(two[h], near[h][0][: RING // 4], near[h][1][RING // 4 :]) for h in range(2)])
    own = place(where, [v for h in range(2) for v in (done[h],) + near[h] + far[h]], summed)
    own = [v.reshape(2, RING, 512) for v in own]
    near = ring([(one[h], own[h], own[h]) for h in range(2)])
    far = ring([(one[h], near[h][0][:1], near[h][1][1:]) for h in range(2)])
    trailing = jnp.zeros((16, 256, 512), F32)
    for h, (_, _, me, _, base) in enumerate(axes):
        for d, value in ((0, own[h]), (3, near[h][0]), (1, near[h][1])):
            trailing = lax.dynamic_update_slice(trailing, value, (base - 6 + 2 * ((me + d) % 4), 0, 0))
    trailing = lax.dynamic_update_slice(trailing, rhs_blocks[6:, RING:] - summed, (0, RING, 0))
    for h, (_, _, me, _, base) in enumerate(axes):
        for i in range(2):
            trailing = lax.dynamic_update_slice(trailing, far[h][i], (base - 6 + 2 * ((me + 2) % 4) + i, 0, 0))
    return jnp.stack(solved), trailing


def solution(mesh):
    in_specs = (P(None, "prow", None), P(None, "prow", None, "pcol"), P(), P(None, None, "prow"))
    out_specs = (P(None, "pcol", None), P(None, "prow", None))
    return jax.shard_map(
        on_device, mesh=mesh, in_specs=in_specs, out_specs=out_specs, check_vma=False
    )
```

```python
import functools

import jax
import jax.numpy as jnp
from jax import lax
from jax.experimental import pallas as pl
from jax.experimental.pallas import tpu as pltpu
from jax.sharding import PartitionSpec as P

F32 = jnp.float32
BF16 = jnp.bfloat16
STEPS = 6
RING = 160
V, H, S = (pl.BlockSpec(memory_space=m) for m in (pltpu.VMEM, pltpu.HBM, pltpu.SMEM))


def split(value):
    high = value.astype(BF16)
    return high, (value - high.astype(F32)).astype(BF16)


def dot(a, b):
    return jnp.dot(a, b, preferred_element_type=F32)


def call(kernel, name, mib, inputs, outputs, scratch=(), blocks=0):
    specs, operands = zip(*inputs)
    return pl.pallas_call(
        kernel,
        in_specs=specs,
        out_specs=[V] * len(outputs),
        out_shape=[jax.ShapeDtypeStruct(*o) for o in outputs],
        scratch_shapes=scratch,
        compiler_params=pltpu.CompilerParams(vmem_limit_bytes=mib << 20),
        cost_estimate=pl.CostEstimate(flops=0, bytes_accessed=blocks << 22, transcendentals=0) if blocks else None,
        name=name,
    )(*operands)


def fetch(pairs, sems):
    copies = [pltpu.make_async_copy(a, b, sems.at[i]) for i, (a, b) in enumerate(pairs)]
    for copy in copies:
        copy.start()
    return copies


def gram_kernel(rows, extra, whole, meta, scale, inverse, rhs, tiles, *refs):
    outs = refs[-7:-6] if whole else refs[-8:-6]
    refs[-6][...] = jnp.zeros((8, 128), F32)
    d_buf, r_buf, t_buf, product, sems = refs[-5:]
    c, y, u = meta[0], meta[1], meta[2]
    blocks = extra + rows
    copies = []
    sem = 0
    for i, b in enumerate(blocks):
        copies.append(fetch([(inverse.at[b], d_buf.at[i]), (rhs.at[b], r_buf.at[i])], sems.at[pl.ds(sem, 2)]))
        sem += 2
    base = 0
    for s in rows:
        copies[len(extra) + rows.index(s)] += fetch(
            [(tiles.at[s, pl.ds(0, s)], t_buf.at[pl.ds(base, s)])], sems.at[pl.ds(sem, 1)]
        )
        sem += 1
        base += s

    def store(slot, row, at):
        for yy in range(4):
            if whole:
                for core in range(2):
                    outs[0][2 * yy + core, at] = product[slot, pl.ds(row + yy * 32 + core * 16, 16), :]
            else:
                ey = lax.rem(yy + 4 - y, 4)
                start = row + yy * 32
                outs[0][ey, at] = product[slot, pl.ds(pl.multiple_of(start + u * 16, 16), 16), :]
                outs[1][ey, at] = product[slot, pl.ds(pl.multiple_of(start + (1 - u) * 16, 16), 16), :]

    turn = 0
    base = 0
    unit = 4 * len(blocks)
    for i, b in enumerate(blocks):
        for copy in copies[i]:
            copy.wait()
        high, low = split(r_buf[i])
        both = jnp.concatenate([high, low], axis=0)
        part = d_buf[i, pl.ds(pl.multiple_of(c * 128, 128), 128), :]
        value = dot(jnp.concatenate([part, part], axis=1), both)
        slot = turn % 2
        turn += 1
        for g in range(4):
            product[slot, pl.ds(g * 128, 128), :] = value[:, g * 128 : (g + 1) * 128]
            store(slot, g * 128, i * 4 + g)
        if b not in rows:
            continue
        for j in range(b):
            slot = turn % 2
            turn += 1
            product[slot] = dot(d_buf[i], t_buf[base]) * scale[j, b]
            base += 1
            for chunk in range(16):
                store(slot, chunk * 128, unit + chunk)
            unit += 16


def gram(rows, extra, whole, meta, scale, inverse, rhs, tiles, *after):
    n = len(extra) + len(rows)
    units = 4 * n + 16 * sum(rows)
    outputs = [((8, units, 16, 128), F32)] if whole else [((4, units, 16, 128), F32)] * 2
    outputs.append(((8, 128), F32))
    return call(
        functools.partial(gram_kernel, rows, extra, whole),
        "gram",
        58,
        [(S, meta), (S, scale), (H, inverse), (H, rhs), (H, tiles)] + [(H, a) for a in after],
        outputs,
        [
            pltpu.VMEM((n, 2048, 256), BF16),
            pltpu.VMEM((n, 256, 512), F32),
            pltpu.VMEM((sum(rows), 256, 128), BF16),
            pltpu.VMEM((2, 2048, 128), F32),
            pltpu.SemaphoreType.DMA((2 * n + len(rows),)),
        ],
        sum(rows) + 2,
    )


def join(meta, pieces, solved, both):
    y, u = meta[1], meta[2]
    for ey in range(4):
        row = lax.rem(y + 4 - ey, 4) * 32
        for eu in range(2):
            at = pl.multiple_of(row + (u + eu - 2 * u * eu) * 16, 16)
            value = pieces[ey][eu]
            high, low = split(value)
            solved[pl.ds(at, 16), :] = value
            both[pl.ds(at, 16), :] = high
            both[pl.ds(pl.multiple_of(at + 128, 16), 16), :] = low


def step_kernel(count, meta, *refs):
    pieces, older, blocks = refs[:4], refs[4 : 3 + count], refs[3 + count]
    terms, solved, both, g_buf, sem = refs[-5:]
    copy = pltpu.make_async_copy(blocks, g_buf, sem)
    copy.start()
    join(meta, pieces, solved, both)
    copy.wait()
    total = None
    for j in range(count):
        high, low = split(g_buf[pl.ds(16 * j, 16)].reshape(256, 128))
        source = both if j == count - 1 else older[j]
        part = dot(jnp.concatenate([high, high], axis=1), source[...]) + dot(low, source[pl.ds(0, 128), :])
        total = part if total is None else total + part
    terms[...] = total.reshape(16, 16, 512)


def step(meta, pieces, older, blocks, after):
    count = len(older) + 1
    return call(
        functools.partial(step_kernel, count),
        "step",
        24,
        [(S, meta)] + [(V, p) for p in pieces] + [(V, o) for o in older] + [(H, blocks)] + [(H, a) for a in after],
        [((16, 16, 512), F32), ((128, 512), F32), ((256, 512), BF16)],
        [pltpu.VMEM((16 * count, 16, 128), F32), pltpu.SemaphoreType.DMA],
    )


def last_kernel(meta, a, b, c, d, solved, both):
    join(meta, (a, b, c, d), solved, both)


def last(meta, pieces):
    inputs = [(S, meta)] + [(V, p) for p in pieces]
    return call(last_kernel, "last", 8, inputs, [((128, 512), F32), ((256, 512), BF16)])


def trail_kernel(groups, adds, first, scale, tiles, *refs):
    both, extras = refs[:STEPS], refs[STEPS : STEPS + len(adds)]
    sems = refs[-1]
    buffers = refs[-1 - len(groups) : -1]
    outs = refs[-1 - len(groups) - sum(len(g[2]) for g in groups) : -1 - len(groups)]
    plan, copies, at = [], [], 0
    for (start, rows, sizes), buffer in zip(groups, buffers):
        count = sum(sizes)
        copies.append(
            fetch(
                [(tiles.at[first[at + i], :, pl.ds(start, rows)], buffer.at[i]) for i in range(count)],
                sems.at[pl.ds(at, count)],
            )
        )
        places = [(out, block) for n, out in zip(sizes, outs) for block in range(n)]
        outs = outs[len(sizes) :]
        plan.append((rows, buffer, places, at))
        at += count
    for (rows, buffer, places, at), waits in zip(plan, copies):
        stack = min(len(places), 8)
        for base in range(0, len(places), stack):
            size = min(stack, len(places) - base)
            for i in range(size):
                waits[base + i].wait()
            for k in range(STEPS):
                own = buffer[pl.ds(base, size), k].reshape(size * rows, 128)
                part = dot(jnp.concatenate([own, own], axis=1), both[k][...])
                for i in range(size):
                    out, block = places[base + i]
                    term = part[i * rows : (i + 1) * rows] * scale[k, first[at + base + i]]
                    out[block] = term if k == 0 else out[block] + term
    outs = refs[-1 - len(groups) - sum(len(g[2]) for g in groups) :]
    for (out, block), ref in zip(adds, extras):
        outs[out][block] += ref[0]


def trail(first, scale, tiles, both, groups, adds=(), extras=(), after=()):
    count = first.shape[0]
    return call(
        functools.partial(trail_kernel, groups, adds),
        "trail",
        56,
        [(S, first), (S, scale), (H, tiles)] + [(V, v) for v in (*both, *extras)] + [(H, a) for a in after],
        [((n, rows, 512), F32) for _, rows, sizes in groups for n in sizes],
        [pltpu.VMEM((sum(sizes), 6, rows, 128), BF16) for _, rows, sizes in groups] + [pltpu.SemaphoreType.DMA((count,))],
        max(1, sum(rows * sum(sizes) for _, rows, sizes in groups) // 256),
    )


def sum_sub_kernel(where, *refs):
    for h in range(2):
        a, b, c = refs[3 * h : 3 * h + 3]
        outs = refs[6 + 5 * h : 11 + 5 * h]

        def rows(e):
            at = lax.rem(where[h] + e, 4)
            return a[at] + (b[at] + c[at])

        outs[0][...] = rows(0)
        outs[1][...] = rows(1)
        outs[2][...] = rows(3)
        far = rows(2)
        outs[3][...] = far[: RING // 4]
        outs[4][...] = far[RING // 4 :]


def sum_sub(where, parts):
    outputs = [((RING // 2, 512), F32)] * 3 + [((RING // 4, 512), F32)] * 2
    return call(sum_sub_kernel, "sum_sub", 32, [(S, where)] + [(V, p) for p in parts], outputs * 2)


def place_kernel(where, *refs):
    for h in range(2):
        own, back, ahead, low, high = refs[5 * h : 5 * h + 5]
        out = refs[10 + h]
        for e, ref in ((0, own), (3, back), (1, ahead)):
            out[lax.rem(where[h] + e, 4)] = ref[...]
        far = lax.rem(where[h] + 2, 4)
        out[far, pl.ds(0, RING // 4), :] = low[...]
        out[far, pl.ds(RING // 4, RING // 4), :] = high[...]


def place(where, parts):
    return call(place_kernel, "place", 16, [(S, where)] + [(V, p) for p in parts], [((4, RING // 2, 512), F32)] * 2)


def write_kernel(count, starts, *refs):
    values, out, sems = refs[:count], refs[-2], refs[-1]
    rows = pl.ds(0, RING)
    copies = fetch(
        [(value, out.at[pl.ds(starts[i], value.shape[0]), rows]) for i, value in enumerate(values)], sems
    )
    for copy in copies:
        copy.wait()


def write(starts, values, out):
    count = len(values)
    return pl.pallas_call(
        functools.partial(write_kernel, count),
        in_specs=[S] + [V] * count + [H],
        out_specs=H,
        out_shape=jax.ShapeDtypeStruct((16, 256, 512), F32),
        scratch_shapes=[pltpu.SemaphoreType.DMA((count,))],
        compiler_params=pltpu.CompilerParams(vmem_limit_bytes=58 << 20),
        input_output_aliases={count + 1: 0},
        name="write",
    )(starts, *values, out)


def rest_kernel(rhs, summed, out, r_buf, s_buf, sems):
    rows = pl.ds(RING, 256 - RING)

    def loads(n):
        slot = n % 2
        return (
            pltpu.make_async_copy(rhs.at[pl.ds(6 + 2 * n, 2), rows], r_buf.at[slot], sems.at[slot]),
            pltpu.make_async_copy(summed.at[pl.ds(2 * n, 2)], s_buf.at[slot], sems.at[2 + slot]),
        )

    def store(n):
        slot = n % 2
        return pltpu.make_async_copy(r_buf.at[slot], out.at[pl.ds(2 * n, 2), rows], sems.at[4 + slot])

    for copy in loads(0):
        copy.start()
    for n in range(8):
        if n + 1 < 8:
            if n >= 1:
                store(n - 1).wait()
            for copy in loads(n + 1):
                copy.start()
        for copy in loads(n):
            copy.wait()
        slot = n % 2
        r_buf[slot] = r_buf[slot] - s_buf[slot]
        store(n).start()
    store(6).wait()
    store(7).wait()


def rest(rhs, summed):
    block = pltpu.VMEM((2, 2, 256 - RING, 512), F32)
    return pl.pallas_call(
        rest_kernel,
        in_specs=[H, H],
        out_specs=H,
        out_shape=jax.ShapeDtypeStruct((16, 256, 512), F32),
        scratch_shapes=[block, block, pltpu.SemaphoreType.DMA((6,))],
        compiler_params=pltpu.CompilerParams(vmem_limit_bytes=58 << 20),
        name="rest",
    )(rhs, summed)


def on_device(rhs_blocks, factor_tiles, tile_scale, diag_inverse):
    row, column = lax.axis_index("prow"), lax.axis_index("pcol")
    y, u, z, x = row // 2, row % 2, column // 4, column % 4
    meta = jnp.stack([column, y, u]).astype(jnp.int32)
    tiles = jnp.transpose(factor_tiles, (0, 2, 1, 3))
    scale = jnp.transpose(tile_scale)

    def shift(value, axis, d):
        if axis == "x":
            return lax.ppermute(value, "pcol", [(i, i // 4 * 4 + (i + d) % 4) for i in range(16)])
        if axis == "z":
            return lax.ppermute(value, "pcol", [(i, (i + 4 * d) % 16) for i in range(16)])
        if axis == "y":
            return lax.ppermute(value, "prow", [(i, (i + 2 * d) % 8) for i in range(8)])
        return lax.ppermute(value, "prow", [(i, i ^ 1) for i in range(8)])

    def exchange(values, axis):
        return [values[0]] + [shift(values[d], axis, d) for d in (1, 2, 3)]

    def spread(value, axis):
        return exchange([value] * 4, axis)

    def ring(values):
        return [(shift(up, axis, 1), shift(down, axis, 3)) for axis, up, down in values]

    def make(rows, extra, whole, *after):
        return gram(rows, extra, whole, meta, scale, diag_inverse, rhs_blocks, tiles, *after)

    def gather(piece):
        both = jnp.stack([piece, shift(piece, "core", 1)])
        return spread(both, "y")

    def ends(total, blocks):
        for i, b in enumerate(blocks):
            start[b] = jnp.transpose(total[4 * i : 4 * i + 4], (1, 0, 2)).reshape(16, 512)

    start, grams = {}, {}
    keep, send, token = make((1,), (0,), False)
    half = keep + shift(send, "core", 1)
    a, b, c, d = exchange([half[i] for i in range(4)], "y")
    total = (a + b) + (c + d)
    ends(total, (0, 1))
    grams[1] = total[8:]
    for rows in ((2, 3), (4, 5)):
        products, token = make(rows, (), True, token, *(() if rows[0] == 2 else (b,)))
        total = lax.psum_scatter(products, "prow")
        ends(total, rows)
        grams[rows[0]], grams[rows[1]] = total[8 : 8 + 16 * rows[0]], total[8 + 16 * rows[0] :]

    solved, both = [], []
    piece = start[0]
    for s in range(1, STEPS):
        terms, latest, parts = step(meta, gather(piece), both, grams[s], (token,) if s == 1 else ())
        solved.append(latest)
        both.append(parts)
        terms = lax.all_to_all(terms, "pcol", 0, 0)
        piece = start[s] - jnp.sum(terms, axis=0)
    latest, parts = last(meta, gather(piece))
    solved.append(latest)
    both.append(parts)

    axes = (("x", "z", x, z, 6), ("z", "x", z, x, 14))
    one, two = [a[0] for a in axes], [a[1] for a in axes]
    where = jnp.stack([a[3] for a in axes]).astype(jnp.int32)

    def chunks_of(offsets):
        return [base + 2 * ((me + d) % 4) + i for d in offsets for _, _, me, _, base in axes for i in range(2)]

    def stacked(values):
        return jnp.stack(values).astype(jnp.int32)

    far = trail(stacked(chunks_of((2,))), scale, tiles, both, ((0, RING, (1,) * 4),))
    moved = ring([(one[h], far[2 * h], far[2 * h + 1]) for h in range(2)])
    shared = trail(jnp.arange(6, 22, dtype=jnp.int32), scale, tiles, both, ((RING, 256 - RING, (16,)),), after=far[:1])[0]
    summed = lax.psum(shared, "pcol")
    own = trail(stacked(chunks_of((0,))), scale, tiles, both, ((0, RING, (2,) * 2),), after=(shared,))
    adds, extras = ((0, 0), (1, 0), (2, 1), (3, 1)), (moved[0][0], moved[1][0], moved[0][1], moved[1][1])
    near = trail(stacked(chunks_of((1, 3))), scale, tiles, both, ((0, RING, (2,) * 4),), adds, extras, own[:1])
    ups, downs = near[:2], near[2:]
    moved = ring([(one[h], ups[h], downs[h]) for h in range(2)])
    terms = [v.reshape(4, RING // 2, 512) for h in range(2) for v in (own[h],) + moved[h]]
    subs = sum_sub(where, terms)
    subs = [subs[:5], subs[5:]]
    moved = ring([(two[h], subs[h][3], subs[h][4]) for h in range(2)])
    ups = [subs[h][1].at[: RING // 4].add(moved[h][0]) for h in range(2)]
    downs = [subs[h][2].at[RING // 4 :].add(moved[h][1]) for h in range(2)]
    moved = ring([(two[h], ups[h], downs[h]) for h in range(2)])
    done = []
    for h, (_, _, me, other, base) in enumerate(axes):
        at = (base + 2 * me + other // 2, other % 2 * (RING // 2), 0)
        mine = lax.dynamic_slice(rhs_blocks, at, (1, RING // 2, 512))[0]
        done.append(mine - (subs[h][0] + (moved[h][0] + moved[h][1])))
    near = ring([(two[h], done[h], done[h]) for h in range(2)])
    far = ring([(two[h], near[h][0][: RING // 4], near[h][1][RING // 4 :]) for h in range(2)])
    own = place(where, [v for h in range(2) for v in (done[h],) + near[h] + far[h]])
    own = [v.reshape(2, RING, 512) for v in own]
    near = ring([(one[h], own[h], own[h]) for h in range(2)])
    far = ring([(one[h], near[h][0][:1], near[h][1][1:]) for h in range(2)])
    trailing = rest(rhs_blocks, summed)
    at = [base - 6 + 2 * ((me + d) % 4) for _, _, me, _, base in axes for d in (0, 3, 1)]
    trailing = write(stacked(at), [v for h in range(2) for v in (own[h],) + near[h]], trailing)
    at = [base - 6 + 2 * ((me + 2) % 4) + i for _, _, me, _, base in axes for i in range(2)]
    trailing = write(stacked(at), [v for h in range(2) for v in far[h]], trailing)
    return jnp.stack(solved), trailing


def solution(mesh):
    in_specs = (P(None, "prow", None), P(None, "prow", None, "pcol"), P(), P(None, None, "prow"))
    out_specs = (P(None, "pcol", None), P(None, "prow", None))
    return jax.shard_map(
        on_device, mesh=mesh, in_specs=in_specs, out_specs=out_specs, check_vma=False
    )
```

```python
import functools

import jax
import jax.numpy as jnp
from jax import lax
from jax.experimental import pallas as pl
from jax.experimental.pallas import tpu as pltpu
from jax.sharding import PartitionSpec as P

F32 = jnp.float32
BF16 = jnp.bfloat16
STEPS = 6
RING = 128
V, H, S = (pl.BlockSpec(memory_space=m) for m in (pltpu.VMEM, pltpu.HBM, pltpu.SMEM))


def split(value):
    high = value.astype(BF16)
    return high, (value - high.astype(F32)).astype(BF16)


def dot(a, b):
    return jnp.dot(a, b, preferred_element_type=F32)


def call(kernel, name, mib, inputs, outputs, scratch=(), blocks=0):
    specs, operands = zip(*inputs)
    return pl.pallas_call(
        kernel,
        in_specs=specs,
        out_specs=[V] * len(outputs),
        out_shape=[jax.ShapeDtypeStruct(*o) for o in outputs],
        scratch_shapes=scratch,
        compiler_params=pltpu.CompilerParams(vmem_limit_bytes=mib << 20),
        cost_estimate=pl.CostEstimate(flops=0, bytes_accessed=blocks << 22, transcendentals=0) if blocks else None,
        name=name,
    )(*operands)


def fetch(pairs, sems):
    copies = [pltpu.make_async_copy(a, b, sems.at[i]) for i, (a, b) in enumerate(pairs)]
    for copy in copies:
        copy.start()
    return copies


def gram_kernel(rows, extra, whole, meta, scale, inverse, rhs, tiles, *refs):
    outs = refs[-7:-6] if whole else refs[-8:-6]
    refs[-6][...] = jnp.zeros((8, 128), F32)
    d_buf, r_buf, t_buf, product, sems = refs[-5:]
    c, y, u = meta[0], meta[1], meta[2]
    blocks = extra + rows
    copies = []
    sem = 0
    for i, b in enumerate(blocks):
        copies.append(fetch([(inverse.at[b], d_buf.at[i]), (rhs.at[b], r_buf.at[i])], sems.at[pl.ds(sem, 2)]))
        sem += 2
    base = 0
    for s in rows:
        copies[len(extra) + rows.index(s)] += fetch(
            [(tiles.at[s, pl.ds(0, s)], t_buf.at[pl.ds(base, s)])], sems.at[pl.ds(sem, 1)]
        )
        sem += 1
        base += s

    def store(slot, row, at):
        for yy in range(4):
            if whole:
                for core in range(2):
                    outs[0][2 * yy + core, at] = product[slot, pl.ds(row + yy * 32 + core * 16, 16), :]
            else:
                ey = lax.rem(yy + 4 - y, 4)
                start = row + yy * 32
                outs[0][ey, at] = product[slot, pl.ds(pl.multiple_of(start + u * 16, 16), 16), :]
                outs[1][ey, at] = product[slot, pl.ds(pl.multiple_of(start + (1 - u) * 16, 16), 16), :]

    turn = 0
    base = 0
    unit = 4 * len(blocks)
    for i, b in enumerate(blocks):
        for copy in copies[i]:
            copy.wait()
        high, low = split(r_buf[i])
        both = jnp.concatenate([high, low], axis=0)
        part = d_buf[i, pl.ds(pl.multiple_of(c * 128, 128), 128), :]
        value = dot(jnp.concatenate([part, part], axis=1), both)
        slot = turn % 2
        turn += 1
        for g in range(4):
            product[slot, pl.ds(g * 128, 128), :] = value[:, g * 128 : (g + 1) * 128]
            store(slot, g * 128, i * 4 + g)
        if b not in rows:
            continue
        for j in range(b):
            slot = turn % 2
            turn += 1
            product[slot] = dot(d_buf[i], t_buf[base]) * scale[j, b]
            base += 1
            for chunk in range(16):
                store(slot, chunk * 128, unit + chunk)
            unit += 16


def gram(rows, extra, whole, meta, scale, inverse, rhs, tiles, *after):
    n = len(extra) + len(rows)
    units = 4 * n + 16 * sum(rows)
    outputs = [((8, units, 16, 128), F32)] if whole else [((4, units, 16, 128), F32)] * 2
    outputs.append(((8, 128), F32))
    return call(
        functools.partial(gram_kernel, rows, extra, whole),
        "gram",
        58,
        [(S, meta), (S, scale), (H, inverse), (H, rhs), (H, tiles)] + [(H, a) for a in after],
        outputs,
        [
            pltpu.VMEM((n, 2048, 256), BF16),
            pltpu.VMEM((n, 256, 512), F32),
            pltpu.VMEM((sum(rows), 256, 128), BF16),
            pltpu.VMEM((2, 2048, 128), F32),
            pltpu.SemaphoreType.DMA((2 * n + len(rows),)),
        ],
        sum(rows) + 2,
    )


def join(meta, pieces, solved, both):
    y, u = meta[1], meta[2]
    for ey in range(4):
        row = lax.rem(y + 4 - ey, 4) * 32
        for eu in range(2):
            at = pl.multiple_of(row + (u + eu - 2 * u * eu) * 16, 16)
            value = pieces[ey][eu]
            high, low = split(value)
            solved[pl.ds(at, 16), :] = value
            both[pl.ds(at, 16), :] = high
            both[pl.ds(pl.multiple_of(at + 128, 16), 16), :] = low


def step_kernel(count, meta, *refs):
    pieces, older, blocks = refs[:4], refs[4 : 3 + count], refs[3 + count]
    terms, solved, both, g_buf, sem = refs[-5:]
    copy = pltpu.make_async_copy(blocks, g_buf, sem)
    copy.start()
    join(meta, pieces, solved, both)
    copy.wait()
    total = None
    for j in range(count):
        high, low = split(g_buf[pl.ds(16 * j, 16)].reshape(256, 128))
        source = both if j == count - 1 else older[j]
        part = dot(jnp.concatenate([high, high], axis=1), source[...]) + dot(low, source[pl.ds(0, 128), :])
        total = part if total is None else total + part
    terms[...] = total.reshape(16, 16, 512)


def step(meta, pieces, older, blocks, after):
    count = len(older) + 1
    return call(
        functools.partial(step_kernel, count),
        "step",
        24,
        [(S, meta)] + [(V, p) for p in pieces] + [(V, o) for o in older] + [(H, blocks)] + [(H, a) for a in after],
        [((16, 16, 512), F32), ((128, 512), F32), ((256, 512), BF16)],
        [pltpu.VMEM((16 * count, 16, 128), F32), pltpu.SemaphoreType.DMA],
    )


def last_kernel(meta, a, b, c, d, solved, both):
    join(meta, (a, b, c, d), solved, both)


def last(meta, pieces):
    inputs = [(S, meta)] + [(V, p) for p in pieces]
    return call(last_kernel, "last", 8, inputs, [((128, 512), F32), ((256, 512), BF16)])


def trail_kernel(groups, adds, first, scale, tiles, *refs):
    both, extras = refs[:STEPS], refs[STEPS : STEPS + len(adds)]
    sems = refs[-1]
    buffers = refs[-1 - len(groups) : -1]
    outs = refs[-1 - len(groups) - sum(len(g[2]) for g in groups) : -1 - len(groups)]
    plan, copies, at = [], [], 0
    for (start, rows, sizes), buffer in zip(groups, buffers):
        count = sum(sizes)
        copies.append(
            fetch(
                [(tiles.at[first[at + i], :, pl.ds(start, rows)], buffer.at[i]) for i in range(count)],
                sems.at[pl.ds(at, count)],
            )
        )
        places = [(out, block) for n, out in zip(sizes, outs) for block in range(n)]
        outs = outs[len(sizes) :]
        plan.append((rows, buffer, places, at))
        at += count
    for (rows, buffer, places, at), waits in zip(plan, copies):
        stack = min(len(places), 8)
        for base in range(0, len(places), stack):
            size = min(stack, len(places) - base)
            for i in range(size):
                waits[base + i].wait()
            for k in range(STEPS):
                own = buffer[pl.ds(base, size), k].reshape(size * rows, 128)
                part = dot(jnp.concatenate([own, own], axis=1), both[k][...])
                for i in range(size):
                    out, block = places[base + i]
                    term = part[i * rows : (i + 1) * rows] * scale[k, first[at + base + i]]
                    out[block] = term if k == 0 else out[block] + term
    outs = refs[-1 - len(groups) - sum(len(g[2]) for g in groups) :]
    for (out, block), ref in zip(adds, extras):
        outs[out][block] += ref[0]


def trail(first, scale, tiles, both, groups, adds=(), extras=(), after=()):
    count = first.shape[0]
    return call(
        functools.partial(trail_kernel, groups, adds),
        "trail",
        56,
        [(S, first), (S, scale), (H, tiles)] + [(V, v) for v in (*both, *extras)] + [(H, a) for a in after],
        [((n, rows, 512), F32) for _, rows, sizes in groups for n in sizes],
        [pltpu.VMEM((sum(sizes), 6, rows, 128), BF16) for _, rows, sizes in groups] + [pltpu.SemaphoreType.DMA((count,))],
    )


def sum_sub_kernel(where, *refs):
    for h in range(2):
        a, b, c = refs[3 * h : 3 * h + 3]
        outs = refs[6 + 5 * h : 11 + 5 * h]

        def rows(e):
            at = lax.rem(where[h] + e, 4)
            return a[at] + (b[at] + c[at])

        outs[0][...] = rows(0)
        outs[1][...] = rows(1)
        outs[2][...] = rows(3)
        far = rows(2)
        outs[3][...] = far[: RING // 4]
        outs[4][...] = far[RING // 4 :]


def sum_sub(where, parts):
    outputs = [((RING // 2, 512), F32)] * 3 + [((RING // 4, 512), F32)] * 2
    return call(sum_sub_kernel, "sum_sub", 32, [(S, where)] + [(V, p) for p in parts], outputs * 2)


def place_kernel(where, *refs):
    for h in range(2):
        own, back, ahead, low, high = refs[5 * h : 5 * h + 5]
        out = refs[10 + h]
        for e, ref in ((0, own), (3, back), (1, ahead)):
            out[lax.rem(where[h] + e, 4)] = ref[...]
        far = lax.rem(where[h] + 2, 4)
        out[far, pl.ds(0, RING // 4), :] = low[...]
        out[far, pl.ds(RING // 4, RING // 4), :] = high[...]


def place(where, parts):
    return call(place_kernel, "place", 16, [(S, where)] + [(V, p) for p in parts], [((4, RING // 2, 512), F32)] * 2)


def forward_kernel(back, ahead, _, up, down, sems):
    copies = fetch([(back.at[pl.ds(0, 1)], up), (ahead.at[pl.ds(1, 1)], down)], sems)
    for copy in copies:
        copy.wait()


def forward(back, ahead, after):
    return call(
        forward_kernel,
        "forward",
        56,
        [(H, back), (H, ahead), (H, after)],
        [((1, RING, 512), F32)] * 2,
        [pltpu.SemaphoreType.DMA((2,))],
    )


def on_device(rhs_blocks, factor_tiles, tile_scale, diag_inverse):
    row, column = lax.axis_index("prow"), lax.axis_index("pcol")
    y, u, z, x = row // 2, row % 2, column // 4, column % 4
    meta = jnp.stack([column, y, u]).astype(jnp.int32)
    tiles = jnp.transpose(factor_tiles, (0, 2, 1, 3))
    scale = jnp.transpose(tile_scale)

    def shift(value, axis, d):
        if axis == "x":
            return lax.ppermute(value, "pcol", [(i, i // 4 * 4 + (i + d) % 4) for i in range(16)])
        if axis == "z":
            return lax.ppermute(value, "pcol", [(i, (i + 4 * d) % 16) for i in range(16)])
        if axis == "y":
            return lax.ppermute(value, "prow", [(i, (i + 2 * d) % 8) for i in range(8)])
        return lax.ppermute(value, "prow", [(i, i ^ 1) for i in range(8)])

    def exchange(values, axis):
        return [values[0]] + [shift(values[d], axis, d) for d in (1, 2, 3)]

    def spread(value, axis):
        return exchange([value] * 4, axis)

    def ring(values):
        return [(shift(up, axis, 1), shift(down, axis, 3)) for axis, up, down in values]

    def make(rows, extra, whole, *after):
        return gram(rows, extra, whole, meta, scale, diag_inverse, rhs_blocks, tiles, *after)

    def gather(piece):
        both = jnp.stack([piece, shift(piece, "core", 1)])
        return spread(both, "y")

    def ends(total, blocks):
        for i, b in enumerate(blocks):
            start[b] = jnp.transpose(total[4 * i : 4 * i + 4], (1, 0, 2)).reshape(16, 512)

    start, grams = {}, {}
    def make_whole(rows, *after):
        total = lax.psum_scatter(make(rows, (), True, *after)[0], "prow")
        ends(total, rows)
        grams[rows[0]], grams[rows[1]] = total[8 : 8 + 16 * rows[0]], total[8 + 16 * rows[0] :]

    keep, send, _ = make((1,), (0,), False)
    half = keep + shift(send, "core", 1)
    a, b, c, d = exchange([half[i] for i in range(4)], "y")
    total = (a + b) + (c + d)
    ends(total, (0, 1))
    grams[1] = total[8:]
    make_whole((2, 3), total)

    solved, both = [], []
    piece = start[0]
    for s in range(1, STEPS):
        terms, latest, parts = step(meta, gather(piece), both, grams[s], ())
        if s == 1:
            make_whole((4, 5), parts)
        solved.append(latest)
        both.append(parts)
        terms = lax.all_to_all(terms, "pcol", 0, 0)
        piece = start[s] - jnp.sum(terms, axis=0)
    latest, parts = last(meta, gather(piece))
    solved.append(latest)
    both.append(parts)

    axes = (("x", "z", x, z, 6), ("z", "x", z, x, 14))
    one, two = [a[0] for a in axes], [a[1] for a in axes]
    where = jnp.stack([a[3] for a in axes]).astype(jnp.int32)

    def chunks_of(offsets):
        return [base + 2 * ((me + d) % 4) + i for d in offsets for _, _, me, _, base in axes for i in range(2)]

    def stacked(values):
        return jnp.stack(values).astype(jnp.int32)

    shared = trail(jnp.arange(6, 22, dtype=jnp.int32), scale, tiles, both, ((RING, 256 - RING, (16,)),))[0]
    summed = lax.psum(shared, "pcol")
    far = trail(stacked(chunks_of((2,))), scale, tiles, both, ((0, RING, (1,) * 4),), after=(shared,))
    moved = ring([(one[h], far[2 * h], far[2 * h + 1]) for h in range(2)])
    adds, extras = ((0, 0), (1, 0), (2, 1), (3, 1)), (moved[0][0], moved[1][0], moved[0][1], moved[1][1])
    near = trail(stacked(chunks_of((1, 3))), scale, tiles, both, ((0, RING, (2,) * 4),), adds, extras)
    own = trail(stacked(chunks_of((0,))), scale, tiles, both, ((0, RING, (2,) * 2),), after=near[:1])
    ups, downs = near[:2], near[2:]
    moved = ring([(one[h], ups[h], downs[h]) for h in range(2)])
    terms = [v.reshape(4, RING // 2, 512) for h in range(2) for v in (own[h],) + moved[h]]
    subs = sum_sub(where, terms)
    subs = [subs[:5], subs[5:]]
    moved = ring([(two[h], subs[h][3], subs[h][4]) for h in range(2)])
    ups = [subs[h][1].at[: RING // 4].add(moved[h][0]) for h in range(2)]
    downs = [subs[h][2].at[RING // 4 :].add(moved[h][1]) for h in range(2)]
    moved = ring([(two[h], ups[h], downs[h]) for h in range(2)])
    done = []
    for h, (_, _, me, other, base) in enumerate(axes):
        at = (base + 2 * me + other // 2, other % 2 * (RING // 2), 0)
        mine = lax.dynamic_slice(rhs_blocks, at, (1, RING // 2, 512))[0]
        done.append(mine - (subs[h][0] + (moved[h][0] + moved[h][1])))
    near = ring([(two[h], done[h], done[h]) for h in range(2)])
    far = ring([(two[h], near[h][0][: RING // 4], near[h][1][RING // 4 :]) for h in range(2)])
    own = place(where, [v for h in range(2) for v in (done[h],) + near[h] + far[h]])
    own = [v.reshape(2, RING, 512) for v in own]
    near = ring([(one[h], own[h], own[h]) for h in range(2)])
    far = ring([(one[h], *forward(*near[h], summed)) for h in range(2)])
    trailing = jnp.zeros((16, 256, 512), F32)
    for h, (_, _, me, _, base) in enumerate(axes):
        for d, value in ((0, own[h]), (3, near[h][0]), (1, near[h][1])):
            trailing = lax.dynamic_update_slice(trailing, value, (base - 6 + 2 * ((me + d) % 4), 0, 0))
    trailing = lax.dynamic_update_slice(trailing, rhs_blocks[6:, RING:] - summed, (0, RING, 0))
    for h, (_, _, me, _, base) in enumerate(axes):
        for i in range(2):
            trailing = lax.dynamic_update_slice(trailing, far[h][i], (base - 6 + 2 * ((me + 2) % 4) + i, 0, 0))
    return jnp.stack(solved), trailing


def solution(mesh):
    in_specs = (P(None, "prow", None), P(None, "prow", None, "pcol"), P(), P(None, None, "prow"))
    out_specs = (P(None, "pcol", None), P(None, "prow", None))
    return jax.shard_map(
        on_device, mesh=mesh, in_specs=in_specs, out_specs=out_specs, check_vma=False
    )
```

```python
import functools

import jax
import jax.numpy as jnp
from jax import lax
from jax.experimental import pallas as pl
from jax.experimental.pallas import tpu as pltpu
from jax.sharding import PartitionSpec as P

F32 = jnp.float32
BF16 = jnp.bfloat16
STEPS = 6
RING = 128
V, H, S = (pl.BlockSpec(memory_space=m) for m in (pltpu.VMEM, pltpu.HBM, pltpu.SMEM))


def split(value):
    high = value.astype(BF16)
    return high, (value - high.astype(F32)).astype(BF16)


def dot(a, b):
    return jnp.dot(a, b, preferred_element_type=F32)


def call(kernel, name, mib, inputs, outputs, scratch=(), blocks=0):
    specs, operands = zip(*inputs)
    return pl.pallas_call(
        kernel,
        in_specs=specs,
        out_specs=[V] * len(outputs),
        out_shape=[jax.ShapeDtypeStruct(*o) for o in outputs],
        scratch_shapes=scratch,
        compiler_params=pltpu.CompilerParams(vmem_limit_bytes=mib << 20),
        cost_estimate=pl.CostEstimate(flops=0, bytes_accessed=blocks << 22, transcendentals=0) if blocks else None,
        name=name,
    )(*operands)


def fetch(pairs, sems):
    copies = [pltpu.make_async_copy(a, b, sems.at[i]) for i, (a, b) in enumerate(pairs)]
    for copy in copies:
        copy.start()
    return copies


def gram_kernel(rows, extra, whole, meta, scale, inverse, rhs, tiles, *refs):
    outs = refs[-7:-6] if whole else refs[-8:-6]
    refs[-6][...] = jnp.zeros((8, 128), F32)
    d_buf, r_buf, t_buf, product, sems = refs[-5:]
    c, y, u = meta[0], meta[1], meta[2]
    blocks = extra + rows
    copies = []
    sem = 0
    for i, b in enumerate(blocks):
        copies.append(fetch([(inverse.at[b], d_buf.at[i]), (rhs.at[b], r_buf.at[i])], sems.at[pl.ds(sem, 2)]))
        sem += 2
    base = 0
    for s in rows:
        copies[len(extra) + rows.index(s)] += fetch(
            [(tiles.at[s, pl.ds(0, s)], t_buf.at[pl.ds(base, s)])], sems.at[pl.ds(sem, 1)]
        )
        sem += 1
        base += s

    def store(slot, row, at):
        for yy in range(4):
            if whole:
                for core in range(2):
                    outs[0][2 * yy + core, at] = product[slot, pl.ds(row + yy * 32 + core * 16, 16), :]
            else:
                ey = lax.rem(yy + 4 - y, 4)
                start = row + yy * 32
                outs[0][ey, at] = product[slot, pl.ds(pl.multiple_of(start + u * 16, 16), 16), :]
                outs[1][ey, at] = product[slot, pl.ds(pl.multiple_of(start + (1 - u) * 16, 16), 16), :]

    turn = 0
    base = 0
    unit = 4 * len(blocks)
    for i, b in enumerate(blocks):
        for copy in copies[i]:
            copy.wait()
        high, low = split(r_buf[i])
        both = jnp.concatenate([high, low], axis=0)
        part = d_buf[i, pl.ds(pl.multiple_of(c * 128, 128), 128), :]
        value = dot(jnp.concatenate([part, part], axis=1), both)
        slot = turn % 2
        turn += 1
        for g in range(4):
            product[slot, pl.ds(g * 128, 128), :] = value[:, g * 128 : (g + 1) * 128]
            store(slot, g * 128, i * 4 + g)
        if b not in rows:
            continue
        if whole:
            for first in range(0, b, 4):
                group = range(first, min(b, first + 4))
                value = dot(d_buf[i], jnp.concatenate([t_buf[base + j] for j in group], axis=1))
                for n, j in enumerate(group):
                    part = value[:, n * 128 : (n + 1) * 128] * scale[j, b]
                    for chunk in range(16):
                        for p in range(8):
                            row = chunk * 128 + p * 16
                            outs[0][p, unit + 16 * j + chunk] = part[row : row + 16]
            base += b
            unit += 16 * b
            continue
        for j in range(b):
            slot = turn % 2
            turn += 1
            product[slot] = dot(d_buf[i], t_buf[base]) * scale[j, b]
            base += 1
            for chunk in range(16):
                store(slot, chunk * 128, unit + chunk)
            unit += 16


def gram(rows, extra, whole, meta, scale, inverse, rhs, tiles, *after):
    n = len(extra) + len(rows)
    units = 4 * n + 16 * sum(rows)
    outputs = [((8, units, 16, 128), F32)] if whole else [((4, units, 16, 128), F32)] * 2
    outputs.append(((8, 128), F32))
    return call(
        functools.partial(gram_kernel, rows, extra, whole),
        "gram",
        58,
        [(S, meta), (S, scale), (H, inverse), (H, rhs), (H, tiles)] + [(H, a) for a in after],
        outputs,
        [
            pltpu.VMEM((n, 2048, 256), BF16),
            pltpu.VMEM((n, 256, 512), F32),
            pltpu.VMEM((sum(rows), 256, 128), BF16),
            pltpu.VMEM((2, 2048, 128), F32),
            pltpu.SemaphoreType.DMA((2 * n + len(rows),)),
        ],
        sum(rows) + 2,
    )


def join(meta, pieces, solved, both):
    y, u = meta[1], meta[2]
    for ey in range(4):
        row = lax.rem(y + 4 - ey, 4) * 32
        for eu in range(2):
            at = pl.multiple_of(row + (u + eu - 2 * u * eu) * 16, 16)
            value = pieces[ey][eu]
            high, low = split(value)
            solved[pl.ds(at, 16), :] = value
            both[pl.ds(at, 16), :] = high
            both[pl.ds(pl.multiple_of(at + 128, 16), 16), :] = low


def step_kernel(count, meta, *refs):
    pieces, older, blocks = refs[:4], refs[4 : 3 + count], refs[3 + count]
    terms, solved, both, g_buf, sem = refs[-5:]
    copy = pltpu.make_async_copy(blocks, g_buf, sem)
    copy.start()
    join(meta, pieces, solved, both)
    copy.wait()
    total = None
    for j in range(count):
        high, low = split(g_buf[pl.ds(16 * j, 16)].reshape(256, 128))
        source = both if j == count - 1 else older[j]
        part = dot(jnp.concatenate([high, high], axis=1), source[...]) + dot(low, source[pl.ds(0, 128), :])
        total = part if total is None else total + part
    terms[...] = total.reshape(16, 16, 512)


def step(meta, pieces, older, blocks, after):
    count = len(older) + 1
    return call(
        functools.partial(step_kernel, count),
        "step",
        24,
        [(S, meta)] + [(V, p) for p in pieces] + [(V, o) for o in older] + [(H, blocks)] + [(H, a) for a in after],
        [((16, 16, 512), F32), ((128, 512), F32), ((256, 512), BF16)],
        [pltpu.VMEM((16 * count, 16, 128), F32), pltpu.SemaphoreType.DMA],
    )


def last_kernel(meta, a, b, c, d, solved, both):
    join(meta, (a, b, c, d), solved, both)


def last(meta, pieces):
    inputs = [(S, meta)] + [(V, p) for p in pieces]
    return call(last_kernel, "last", 8, inputs, [((128, 512), F32), ((256, 512), BF16)])


def trail_kernel(groups, adds, first, scale, tiles, *refs):
    both, extras = refs[:STEPS], refs[STEPS : STEPS + len(adds)]
    sems = refs[-1]
    buffers = refs[-1 - len(groups) : -1]
    outs = refs[-1 - len(groups) - sum(len(g[2]) for g in groups) : -1 - len(groups)]
    plan, copies, at = [], [], 0
    for (start, rows, sizes), buffer in zip(groups, buffers):
        count = sum(sizes)
        copies.append(
            fetch(
                [(tiles.at[first[at + i], :, pl.ds(start, rows)], buffer.at[i]) for i in range(count)],
                sems.at[pl.ds(at, count)],
            )
        )
        places = [(out, block) for n, out in zip(sizes, outs) for block in range(n)]
        outs = outs[len(sizes) :]
        plan.append((rows, buffer, places, at))
        at += count
    for (rows, buffer, places, at), waits in zip(plan, copies):
        stack = min(len(places), 8)
        for base in range(0, len(places), stack):
            size = min(stack, len(places) - base)
            for i in range(size):
                waits[base + i].wait()
            for k in range(STEPS):
                own = buffer[pl.ds(base, size), k].reshape(size * rows, 128)
                part = dot(jnp.concatenate([own, own], axis=1), both[k][...])
                for i in range(size):
                    out, block = places[base + i]
                    term = part[i * rows : (i + 1) * rows] * scale[k, first[at + base + i]]
                    out[block] = term if k == 0 else out[block] + term
    outs = refs[-1 - len(groups) - sum(len(g[2]) for g in groups) :]
    for (out, block), ref in zip(adds, extras):
        outs[out][block] += ref[0]


def trail(first, scale, tiles, both, groups, adds=(), extras=(), after=()):
    count = first.shape[0]
    return call(
        functools.partial(trail_kernel, groups, adds),
        "trail",
        56,
        [(S, first), (S, scale), (H, tiles)] + [(V, v) for v in (*both, *extras)] + [(H, a) for a in after],
        [((n, rows, 512), F32) for _, rows, sizes in groups for n in sizes],
        [pltpu.VMEM((sum(sizes), 6, rows, 128), BF16) for _, rows, sizes in groups] + [pltpu.SemaphoreType.DMA((count,))],
    )


def sum_sub_kernel(where, *refs):
    for h in range(2):
        a, b, c = refs[3 * h : 3 * h + 3]
        outs = refs[6 + 5 * h : 11 + 5 * h]

        def rows(e):
            at = lax.rem(where[h] + e, 4)
            return a[at] + (b[at] + c[at])

        outs[0][...] = rows(0)
        outs[1][...] = rows(1)
        outs[2][...] = rows(3)
        far = rows(2)
        outs[3][...] = far[: RING // 4]
        outs[4][...] = far[RING // 4 :]


def sum_sub(where, parts):
    outputs = [((RING // 2, 512), F32)] * 3 + [((RING // 4, 512), F32)] * 2
    return call(sum_sub_kernel, "sum_sub", 32, [(S, where)] + [(V, p) for p in parts], outputs * 2)


def place_kernel(where, *refs):
    for h in range(2):
        own, back, ahead, low, high = refs[5 * h : 5 * h + 5]
        out = refs[10 + h]
        for e, ref in ((0, own), (3, back), (1, ahead)):
            out[lax.rem(where[h] + e, 4)] = ref[...]
        far = lax.rem(where[h] + 2, 4)
        out[far, pl.ds(0, RING // 4), :] = low[...]
        out[far, pl.ds(RING // 4, RING // 4), :] = high[...]


def place(where, parts):
    return call(place_kernel, "place", 16, [(S, where)] + [(V, p) for p in parts], [((4, RING // 2, 512), F32)] * 2)


def forward_kernel(back, ahead, _, up, down, sems):
    copies = fetch([(back.at[pl.ds(0, 1)], up), (ahead.at[pl.ds(1, 1)], down)], sems)
    for copy in copies:
        copy.wait()


def forward(back, ahead, after):
    return call(
        forward_kernel,
        "forward",
        56,
        [(H, back), (H, ahead), (H, after)],
        [((1, RING, 512), F32)] * 2,
        [pltpu.SemaphoreType.DMA((2,))],
    )


def on_device(rhs_blocks, factor_tiles, tile_scale, diag_inverse):
    row, column = lax.axis_index("prow"), lax.axis_index("pcol")
    y, u, z, x = row // 2, row % 2, column // 4, column % 4
    meta = jnp.stack([column, y, u]).astype(jnp.int32)
    tiles = jnp.transpose(factor_tiles, (0, 2, 1, 3))
    scale = jnp.transpose(tile_scale)

    def shift(value, axis, d):
        if axis == "x":
            return lax.ppermute(value, "pcol", [(i, i // 4 * 4 + (i + d) % 4) for i in range(16)])
        if axis == "z":
            return lax.ppermute(value, "pcol", [(i, (i + 4 * d) % 16) for i in range(16)])
        if axis == "y":
            return lax.ppermute(value, "prow", [(i, (i + 2 * d) % 8) for i in range(8)])
        return lax.ppermute(value, "prow", [(i, i ^ 1) for i in range(8)])

    def exchange(values, axis):
        return [values[0]] + [shift(values[d], axis, d) for d in (1, 2, 3)]

    def spread(value, axis):
        return exchange([value] * 4, axis)

    def ring(values):
        return [(shift(up, axis, 1), shift(down, axis, 3)) for axis, up, down in values]

    def make(rows, extra, whole, *after):
        return gram(rows, extra, whole, meta, scale, diag_inverse, rhs_blocks, tiles, *after)

    def gather(piece):
        both = jnp.stack([piece, shift(piece, "core", 1)])
        return spread(both, "y")

    def ends(total, blocks):
        for i, b in enumerate(blocks):
            start[b] = jnp.transpose(total[4 * i : 4 * i + 4], (1, 0, 2)).reshape(16, 512)

    start, grams = {}, {}
    def make_whole(rows, *after):
        products, token = make(rows, (), True, *after)
        total = lax.psum_scatter(products, "prow")
        ends(total, rows)
        grams[rows[0]], grams[rows[1]] = total[8 : 8 + 16 * rows[0]], total[8 + 16 * rows[0] :]
        return token

    keep, send, _ = make((1,), (0,), False)
    half = keep + shift(send, "core", 1)
    a, b, c, d = exchange([half[i] for i in range(4)], "y")
    total = (a + b) + (c + d)
    ends(total, (0, 1))
    grams[1] = total[8:]
    token = make_whole((4, 5), make_whole((2, 3), total))

    solved, both = [], []
    piece = start[0]
    for s in range(1, STEPS):
        terms, latest, parts = step(meta, gather(piece), both, grams[s], (token,) if s == 1 else ())
        solved.append(latest)
        both.append(parts)
        terms = lax.all_to_all(terms, "pcol", 0, 0)
        piece = start[s] - jnp.sum(terms, axis=0)
    latest, parts = last(meta, gather(piece))
    solved.append(latest)
    both.append(parts)

    axes = (("x", "z", x, z, 6), ("z", "x", z, x, 14))
    one, two = [a[0] for a in axes], [a[1] for a in axes]
    where = jnp.stack([a[3] for a in axes]).astype(jnp.int32)

    def chunks_of(offsets):
        return [base + 2 * ((me + d) % 4) + i for d in offsets for _, _, me, _, base in axes for i in range(2)]

    def stacked(values):
        return jnp.stack(values).astype(jnp.int32)

    shared = trail(jnp.arange(6, 22, dtype=jnp.int32), scale, tiles, both, ((RING, 256 - RING, (16,)),))[0]
    summed = lax.psum(shared, "pcol")
    far = trail(stacked(chunks_of((2,))), scale, tiles, both, ((0, RING, (1,) * 4),), after=(shared,))
    moved = ring([(one[h], far[2 * h], far[2 * h + 1]) for h in range(2)])
    adds, extras = ((0, 0), (1, 0), (2, 1), (3, 1)), (moved[0][0], moved[1][0], moved[0][1], moved[1][1])
    near = trail(stacked(chunks_of((1, 3))), scale, tiles, both, ((0, RING, (2,) * 4),), adds, extras)
    own = trail(stacked(chunks_of((0,))), scale, tiles, both, ((0, RING, (2,) * 2),), after=near[:1])
    ups, downs = near[:2], near[2:]
    moved = ring([(one[h], ups[h], downs[h]) for h in range(2)])
    terms = [v.reshape(4, RING // 2, 512) for h in range(2) for v in (own[h],) + moved[h]]
    subs = sum_sub(where, terms)
    subs = [subs[:5], subs[5:]]
    moved = ring([(two[h], subs[h][3], subs[h][4]) for h in range(2)])
    ups = [subs[h][1].at[: RING // 4].add(moved[h][0]) for h in range(2)]
    downs = [subs[h][2].at[RING // 4 :].add(moved[h][1]) for h in range(2)]
    moved = ring([(two[h], ups[h], downs[h]) for h in range(2)])
    done = []
    for h, (_, _, me, other, base) in enumerate(axes):
        at = (base + 2 * me + other // 2, other % 2 * (RING // 2), 0)
        mine = lax.dynamic_slice(rhs_blocks, at, (1, RING // 2, 512))[0]
        done.append(mine - (subs[h][0] + (moved[h][0] + moved[h][1])))
    near = ring([(two[h], done[h], done[h]) for h in range(2)])
    far = ring([(two[h], near[h][0][: RING // 4], near[h][1][RING // 4 :]) for h in range(2)])
    own = place(where, [v for h in range(2) for v in (done[h],) + near[h] + far[h]])
    own = [v.reshape(2, RING, 512) for v in own]
    near = ring([(one[h], own[h], own[h]) for h in range(2)])
    far = ring([(one[h], *forward(*near[h], summed)) for h in range(2)])
    trailing = jnp.zeros((16, 256, 512), F32)
    for h, (_, _, me, _, base) in enumerate(axes):
        for d, value in ((0, own[h]), (3, near[h][0]), (1, near[h][1])):
            trailing = lax.dynamic_update_slice(trailing, value, (base - 6 + 2 * ((me + d) % 4), 0, 0))
    trailing = lax.dynamic_update_slice(trailing, rhs_blocks[6:, RING:] - summed, (0, RING, 0))
    for h, (_, _, me, _, base) in enumerate(axes):
        for i in range(2):
            trailing = lax.dynamic_update_slice(trailing, far[h][i], (base - 6 + 2 * ((me + 2) % 4) + i, 0, 0))
    return jnp.stack(solved), trailing


def solution(mesh):
    in_specs = (P(None, "prow", None), P(None, "prow", None, "pcol"), P(), P(None, None, "prow"))
    out_specs = (P(None, "pcol", None), P(None, "prow", None))
    return jax.shard_map(
        on_device, mesh=mesh, in_specs=in_specs, out_specs=out_specs, check_vma=False
    )
```

```python
import functools

import jax
import jax.numpy as jnp
from jax import lax
from jax.experimental import pallas as pl
from jax.experimental.pallas import tpu as pltpu
from jax.sharding import PartitionSpec as P

F32 = jnp.float32
BF16 = jnp.bfloat16
STEPS = 6
RING = 128
V, H, S = (pl.BlockSpec(memory_space=m) for m in (pltpu.VMEM, pltpu.HBM, pltpu.SMEM))


def split(value):
    high = value.astype(BF16)
    return high, (value - high.astype(F32)).astype(BF16)


def dot(a, b):
    return jnp.dot(a, b, preferred_element_type=F32)


def call(kernel, name, mib, inputs, outputs, scratch=(), blocks=0):
    specs, operands = zip(*inputs)
    return pl.pallas_call(
        kernel,
        in_specs=specs,
        out_specs=[V] * len(outputs),
        out_shape=[jax.ShapeDtypeStruct(*o) for o in outputs],
        scratch_shapes=scratch,
        compiler_params=pltpu.CompilerParams(vmem_limit_bytes=mib << 20),
        cost_estimate=pl.CostEstimate(flops=0, bytes_accessed=blocks << 22, transcendentals=0) if blocks else None,
        name=name,
    )(*operands)


def fetch(pairs, sems):
    copies = [pltpu.make_async_copy(a, b, sems.at[i]) for i, (a, b) in enumerate(pairs)]
    for copy in copies:
        copy.start()
    return copies


def gram_kernel(rows, extra, whole, meta, scale, inverse, rhs, tiles, *refs):
    outs = refs[-7:-6] if whole else refs[-8:-6]
    refs[-6][...] = jnp.zeros((8, 128), F32)
    d_buf, r_buf, t_buf, product, sems = refs[-5:]
    c, y, u = meta[0], meta[1], meta[2]
    blocks = extra + rows
    copies = []
    sem = 0
    for i, b in enumerate(blocks):
        copies.append(fetch([(inverse.at[b], d_buf.at[i]), (rhs.at[b], r_buf.at[i])], sems.at[pl.ds(sem, 2)]))
        sem += 2
    base = 0
    for s in rows:
        copies[len(extra) + rows.index(s)] += fetch(
            [(tiles.at[s, pl.ds(0, s)], t_buf.at[pl.ds(base, s)])], sems.at[pl.ds(sem, 1)]
        )
        sem += 1
        base += s

    def store(slot, row, at):
        for yy in range(4):
            if whole:
                for core in range(2):
                    outs[0][2 * yy + core, at] = product[slot, pl.ds(row + yy * 32 + core * 16, 16), :]
            else:
                ey = lax.rem(yy + 4 - y, 4)
                start = row + yy * 32
                outs[0][ey, at] = product[slot, pl.ds(pl.multiple_of(start + u * 16, 16), 16), :]
                outs[1][ey, at] = product[slot, pl.ds(pl.multiple_of(start + (1 - u) * 16, 16), 16), :]

    turn = 0
    base = 0
    unit = 4 * len(blocks)
    for i, b in enumerate(blocks):
        for copy in copies[i]:
            copy.wait()
        high, low = split(r_buf[i])
        both = jnp.concatenate([high, low], axis=0)
        part = d_buf[i, pl.ds(pl.multiple_of(c * 128, 128), 128), :]
        value = dot(jnp.concatenate([part, part], axis=1), both)
        slot = turn % 2
        turn += 1
        for g in range(4):
            product[slot, pl.ds(g * 128, 128), :] = value[:, g * 128 : (g + 1) * 128]
            store(slot, g * 128, i * 4 + g)
        if b not in rows:
            continue
        if whole:
            for first in range(0, b, 4):
                group = range(first, min(b, first + 4))
                value = dot(d_buf[i], jnp.concatenate([t_buf[base + j] for j in group], axis=1))
                for n, j in enumerate(group):
                    part = value[:, n * 128 : (n + 1) * 128] * scale[j, b]
                    for chunk in range(16):
                        for p in range(8):
                            row = chunk * 128 + p * 16
                            outs[0][p, unit + 16 * j + chunk] = part[row : row + 16]
            base += b
            unit += 16 * b
            continue
        for j in range(b):
            slot = turn % 2
            turn += 1
            product[slot] = dot(d_buf[i], t_buf[base]) * scale[j, b]
            base += 1
            for chunk in range(16):
                store(slot, chunk * 128, unit + chunk)
            unit += 16


def gram(rows, extra, whole, meta, scale, inverse, rhs, tiles, *after):
    n = len(extra) + len(rows)
    units = 4 * n + 16 * sum(rows)
    outputs = [((8, units, 16, 128), F32)] if whole else [((4, units, 16, 128), F32)] * 2
    outputs.append(((8, 128), F32))
    return call(
        functools.partial(gram_kernel, rows, extra, whole),
        "gram",
        58,
        [(S, meta), (S, scale), (H, inverse), (H, rhs), (H, tiles)] + [(H, a) for a in after],
        outputs,
        [
            pltpu.VMEM((n, 2048, 256), BF16),
            pltpu.VMEM((n, 256, 512), F32),
            pltpu.VMEM((sum(rows), 256, 128), BF16),
            pltpu.VMEM((2, 2048, 128), F32),
            pltpu.SemaphoreType.DMA((2 * n + len(rows),)),
        ],
        sum(rows) + 2,
    )


def join(meta, pieces, solved, both):
    y, u = meta[1], meta[2]
    for ey in range(4):
        row = lax.rem(y + 4 - ey, 4) * 32
        for eu in range(2):
            at = pl.multiple_of(row + (u + eu - 2 * u * eu) * 16, 16)
            value = pieces[ey][eu]
            high, low = split(value)
            solved[pl.ds(at, 16), :] = value
            both[pl.ds(at, 16), :] = high
            both[pl.ds(pl.multiple_of(at + 128, 16), 16), :] = low


def step_kernel(count, meta, *refs):
    pieces, older, blocks = refs[:4], refs[4 : 3 + count], refs[3 + count]
    terms, solved, both, g_buf, sem = refs[-5:]
    copy = pltpu.make_async_copy(blocks, g_buf, sem)
    copy.start()
    join(meta, pieces, solved, both)
    copy.wait()
    total = None
    for j in range(count):
        high, low = split(g_buf[pl.ds(16 * j, 16)].reshape(256, 128))
        source = both if j == count - 1 else older[j]
        part = dot(jnp.concatenate([high, high], axis=1), source[...]) + dot(low, source[pl.ds(0, 128), :])
        total = part if total is None else total + part
    terms[...] = total.reshape(16, 16, 512)


def step(meta, pieces, older, blocks, after):
    count = len(older) + 1
    return call(
        functools.partial(step_kernel, count),
        "step",
        24,
        [(S, meta)] + [(V, p) for p in pieces] + [(V, o) for o in older] + [(H, blocks)] + [(H, a) for a in after],
        [((16, 16, 512), F32), ((128, 512), F32), ((256, 512), BF16)],
        [pltpu.VMEM((16 * count, 16, 128), F32), pltpu.SemaphoreType.DMA],
    )


def last_kernel(meta, a, b, c, d, solved, both):
    join(meta, (a, b, c, d), solved, both)


def last(meta, pieces):
    inputs = [(S, meta)] + [(V, p) for p in pieces]
    return call(last_kernel, "last", 8, inputs, [((128, 512), F32), ((256, 512), BF16)])


def trail_kernel(groups, adds, first, scale, tiles, *refs):
    both, extras = refs[:STEPS], refs[STEPS : STEPS + len(adds)]
    sems = refs[-1]
    buffers = refs[-1 - len(groups) : -1]
    outs = refs[-1 - len(groups) - sum(len(g[2]) for g in groups) : -1 - len(groups)]
    plan, copies, at = [], [], 0
    for (start, rows, sizes), buffer in zip(groups, buffers):
        count = sum(sizes)
        copies.append(
            fetch(
                [(tiles.at[first[at + i], :, pl.ds(start, rows)], buffer.at[i]) for i in range(count)],
                sems.at[pl.ds(at, count)],
            )
        )
        places = [(out, block) for n, out in zip(sizes, outs) for block in range(n)]
        outs = outs[len(sizes) :]
        plan.append((rows, buffer, places, at))
        at += count
    for (rows, buffer, places, at), waits in zip(plan, copies):
        stack = min(len(places), 8)
        for base in range(0, len(places), stack):
            size = min(stack, len(places) - base)
            for i in range(size):
                waits[base + i].wait()
            for k in range(STEPS):
                own = buffer[pl.ds(base, size), k].reshape(size * rows, 128)
                part = dot(jnp.concatenate([own, own], axis=1), both[k][...])
                for i in range(size):
                    out, block = places[base + i]
                    term = part[i * rows : (i + 1) * rows] * scale[k, first[at + base + i]]
                    out[block] = term if k == 0 else out[block] + term
    outs = refs[-1 - len(groups) - sum(len(g[2]) for g in groups) :]
    for (out, block), ref in zip(adds, extras):
        outs[out][block] += ref[0]


def trail(first, scale, tiles, both, groups, adds=(), extras=(), after=()):
    count = first.shape[0]
    return call(
        functools.partial(trail_kernel, groups, adds),
        "trail",
        56,
        [(S, first), (S, scale), (H, tiles)] + [(V, v) for v in (*both, *extras)] + [(H, a) for a in after],
        [((n, rows, 512), F32) for _, rows, sizes in groups for n in sizes],
        [pltpu.VMEM((sum(sizes), 6, rows, 128), BF16) for _, rows, sizes in groups] + [pltpu.SemaphoreType.DMA((count,))],
    )


def sum_sub_kernel(where, *refs):
    for h in range(2):
        a, b, c = refs[3 * h : 3 * h + 3]
        outs = refs[6 + 5 * h : 11 + 5 * h]

        def rows(e):
            at = lax.rem(where[h] + e, 4)
            return a[at] + (b[at] + c[at])

        outs[0][...] = rows(0)
        outs[1][...] = rows(1)
        outs[2][...] = rows(3)
        far = rows(2)
        outs[3][...] = far[: RING // 4]
        outs[4][...] = far[RING // 4 :]


def sum_sub(where, parts):
    outputs = [((RING // 2, 512), F32)] * 3 + [((RING // 4, 512), F32)] * 2
    return call(sum_sub_kernel, "sum_sub", 32, [(S, where)] + [(V, p) for p in parts], outputs * 2)


def place_kernel(where, *refs):
    for h in range(2):
        own, back, ahead, low, high = refs[5 * h : 5 * h + 5]
        out = refs[10 + h]
        for e, ref in ((0, own), (3, back), (1, ahead)):
            out[lax.rem(where[h] + e, 4)] = ref[...]
        far = lax.rem(where[h] + 2, 4)
        out[far, pl.ds(0, RING // 4), :] = low[...]
        out[far, pl.ds(RING // 4, RING // 4), :] = high[...]


def place(where, parts):
    return call(place_kernel, "place", 16, [(S, where)] + [(V, p) for p in parts], [((4, RING // 2, 512), F32)] * 2)


def forward_kernel(back, ahead, _, up, down, sems):
    copies = fetch([(back.at[pl.ds(0, 1)], up), (ahead.at[pl.ds(1, 1)], down)], sems)
    for copy in copies:
        copy.wait()


def forward(back, ahead, after):
    return call(
        forward_kernel,
        "forward",
        56,
        [(H, back), (H, ahead), (H, after)],
        [((1, RING, 512), F32)] * 2,
        [pltpu.SemaphoreType.DMA((2,))],
    )


def on_device(rhs_blocks, factor_tiles, tile_scale, diag_inverse):
    row, column = lax.axis_index("prow"), lax.axis_index("pcol")
    y, u, z, x = row // 2, row % 2, column // 4, column % 4
    meta = jnp.stack([column, y, u]).astype(jnp.int32)
    tiles = jnp.transpose(factor_tiles, (0, 2, 1, 3))
    scale = jnp.transpose(tile_scale)

    def shift(value, axis, d):
        if axis == "x":
            return lax.ppermute(value, "pcol", [(i, i // 4 * 4 + (i + d) % 4) for i in range(16)])
        if axis == "z":
            return lax.ppermute(value, "pcol", [(i, (i + 4 * d) % 16) for i in range(16)])
        if axis == "y":
            return lax.ppermute(value, "prow", [(i, (i + 2 * d) % 8) for i in range(8)])
        return lax.ppermute(value, "prow", [(i, i ^ 1) for i in range(8)])

    def exchange(values, axis):
        return [values[0]] + [shift(values[d], axis, d) for d in (1, 2, 3)]

    def spread(value, axis):
        return exchange([value] * 4, axis)

    def ring(values):
        return [(shift(up, axis, 1), shift(down, axis, 3)) for axis, up, down in values]

    def make(rows, extra, whole, *after):
        return gram(rows, extra, whole, meta, scale, diag_inverse, rhs_blocks, tiles, *after)

    def gather(piece):
        both = jnp.stack([piece, shift(piece, "core", 1)])
        return spread(both, "y")

    def ends(total, blocks):
        for i, b in enumerate(blocks):
            start[b] = jnp.transpose(total[4 * i : 4 * i + 4], (1, 0, 2)).reshape(16, 512)

    start, grams = {}, {}
    def make_whole(rows, *after):
        products, token = make(rows, (), True, *after)
        total = lax.psum_scatter(products, "prow")
        ends(total, rows)
        at = 4 * len(rows)
        for s in rows:
            grams[s] = total[at : at + 16 * s]
            at += 16 * s
        return token

    keep, send, _ = make((1,), (0,), False)
    half = keep + shift(send, "core", 1)
    a, b, c, d = exchange([half[i] for i in range(4)], "y")
    total = (a + b) + (c + d)
    ends(total, (0, 1))
    grams[1] = total[8:]
    token = make_whole((5,), make_whole((4,), make_whole((2, 3), total)))

    solved, both = [], []
    piece = start[0]
    for s in range(1, STEPS):
        terms, latest, parts = step(meta, gather(piece), both, grams[s], (token,) if s == 1 else ())
        solved.append(latest)
        both.append(parts)
        terms = lax.all_to_all(terms, "pcol", 0, 0)
        piece = start[s] - jnp.sum(terms, axis=0)
    latest, parts = last(meta, gather(piece))
    solved.append(latest)
    both.append(parts)

    axes = (("x", "z", x, z, 6), ("z", "x", z, x, 14))
    one, two = [a[0] for a in axes], [a[1] for a in axes]
    where = jnp.stack([a[3] for a in axes]).astype(jnp.int32)

    def chunks_of(offsets):
        return [base + 2 * ((me + d) % 4) + i for d in offsets for _, _, me, _, base in axes for i in range(2)]

    def stacked(values):
        return jnp.stack(values).astype(jnp.int32)

    shared = trail(jnp.arange(6, 22, dtype=jnp.int32), scale, tiles, both, ((RING, 256 - RING, (16,)),))[0]
    summed = lax.psum(shared, "pcol")
    far = trail(stacked(chunks_of((2,))), scale, tiles, both, ((0, RING, (1,) * 4),), after=(shared,))
    moved = ring([(one[h], far[2 * h], far[2 * h + 1]) for h in range(2)])
    adds, extras = ((0, 0), (1, 0), (2, 1), (3, 1)), (moved[0][0], moved[1][0], moved[0][1], moved[1][1])
    near = trail(stacked(chunks_of((1, 3))), scale, tiles, both, ((0, RING, (2,) * 4),), adds, extras)
    own = trail(stacked(chunks_of((0,))), scale, tiles, both, ((0, RING, (2,) * 2),), after=near[:1])
    ups, downs = near[:2], near[2:]
    moved = ring([(one[h], ups[h], downs[h]) for h in range(2)])
    terms = [v.reshape(4, RING // 2, 512) for h in range(2) for v in (own[h],) + moved[h]]
    subs = sum_sub(where, terms)
    subs = [subs[:5], subs[5:]]
    moved = ring([(two[h], subs[h][3], subs[h][4]) for h in range(2)])
    ups = [subs[h][1].at[: RING // 4].add(moved[h][0]) for h in range(2)]
    downs = [subs[h][2].at[RING // 4 :].add(moved[h][1]) for h in range(2)]
    moved = ring([(two[h], ups[h], downs[h]) for h in range(2)])
    done = []
    for h, (_, _, me, other, base) in enumerate(axes):
        at = (base + 2 * me + other // 2, other % 2 * (RING // 2), 0)
        mine = lax.dynamic_slice(rhs_blocks, at, (1, RING // 2, 512))[0]
        done.append(mine - (subs[h][0] + (moved[h][0] + moved[h][1])))
    near = ring([(two[h], done[h], done[h]) for h in range(2)])
    far = ring([(two[h], near[h][0][: RING // 4], near[h][1][RING // 4 :]) for h in range(2)])
    own = place(where, [v for h in range(2) for v in (done[h],) + near[h] + far[h]])
    own = [v.reshape(2, RING, 512) for v in own]
    near = ring([(one[h], own[h], own[h]) for h in range(2)])
    far = ring([(one[h], *forward(*near[h], summed)) for h in range(2)])
    trailing = jnp.zeros((16, 256, 512), F32)
    for h, (_, _, me, _, base) in enumerate(axes):
        for d, value in ((0, own[h]), (3, near[h][0]), (1, near[h][1])):
            trailing = lax.dynamic_update_slice(trailing, value, (base - 6 + 2 * ((me + d) % 4), 0, 0))
    trailing = lax.dynamic_update_slice(trailing, rhs_blocks[6:, RING:] - summed, (0, RING, 0))
    for h, (_, _, me, _, base) in enumerate(axes):
        for i in range(2):
            trailing = lax.dynamic_update_slice(trailing, far[h][i], (base - 6 + 2 * ((me + 2) % 4) + i, 0, 0))
    return jnp.stack(solved), trailing


def solution(mesh):
    in_specs = (P(None, "prow", None), P(None, "prow", None, "pcol"), P(), P(None, None, "prow"))
    out_specs = (P(None, "pcol", None), P(None, "prow", None))
    return jax.shard_map(
        on_device, mesh=mesh, in_specs=in_specs, out_specs=out_specs, check_vma=False
    )
```
